32 devices in a mesh: fsdp: 16 (over z, x, core), seq: 2 (over y).
Axes of the slice: x: 2, y: 2, z: 4, core: 2. Of those that a mesh axis runs over, the one named last changes fastest.
Arguments:
- tokens: bfloat16 [16, 1024, 1152], P('fsdp', 'seq'), may hold values from -6 to 6
- lengths: int32 [16], P('fsdp'), may hold values from 128 to 1024, as said below
- cotangent: bfloat16 [16, 1024, 1152], P('fsdp', 'seq'), may hold values from -6 to 6
- attn_gain: float32 [1152], replicated, may hold values from 0.25 to 1.75
- attn_shift: float32 [1152], replicated, may hold values from -2 to 2
- qkv_weight: bfloat16 [1152, 3456], P('fsdp'), may hold values from -0.1875 to 0.1875
- query_bias: float32 [1152], replicated, may hold values from -3 to 3
- value_bias: float32 [1152], replicated, may hold values from -3 to 3
- out_weight: bfloat16 [1152, 1152], P('fsdp'), may hold values from -3 to 3
- out_bias: float32 [1152], replicated, may hold values from -2 to 2
- mlp_gain: float32 [1152], replicated, may hold values from 0.25 to 1.75
- mlp_shift: float32 [1152], replicated, may hold values from -2 to 2
- up_weight: bfloat16 [1152, 4304], P('fsdp'), may hold values from -0.1875 to 0.1875
- up_bias: float32 [4304], replicated, may hold values from -3 to 3
- down_weight: bfloat16 [4304, 1152], P(None, 'fsdp'), may hold values from -0.09375 to 0.09375
- down_bias: float32 [1152], replicated, may hold values from -2 to 2
Outputs:
- outputs: bfloat16 [16, 1024, 1152], P('fsdp', 'seq')
- grad_tokens: float32 [16, 1024, 1152], P('fsdp', 'seq')
- grad_attn_gain: float32 [1152], replicated
- grad_attn_shift: float32 [1152], replicated
- grad_qkv: float32 [1152, 3456], P('fsdp')
- grad_query_bias: float32 [1152], replicated
- grad_value_bias: float32 [1152], replicated
- grad_out: float32 [1152, 1152], P('fsdp')
- grad_out_bias: float32 [1152], replicated
- grad_mlp_gain: float32 [1152], replicated
- grad_mlp_shift: float32 [1152], replicated
- grad_up: float32 [1152, 4304], P('fsdp')
- grad_up_bias: float32 [4304], replicated
- grad_down: float32 [4304, 1152], P(None, 'fsdp')
- grad_down_bias: float32 [1152], replicated
The draws below stay inside these ranges and needn't reach their ends.
Inputs may be any that keep to these rules, and one draw needn't show every extreme that they name: `lengths`: of the 1 images of each fsdp index, one has at least 960 valid tokens.
All inputs are finite; a program needn't handle non-finite values.
Results may differ from the reference program's by a relative error of at most 0.015.
Values may be sent and summed in bfloat16 or wider, within the bound.
No kernel may reach another device: no remote copies, remote signals or barrier semaphores. Data moves between devices by JAX's collectives and lax.ppermute only.
A program may use at most 256 MiB of HBM per device.

```python
import jax
import jax.numpy as jnp
from jax import lax

D = 1152
HEADS = 16
HD = 72
FF = 4304
LEN = 1024
IMGS = 1
IMAGES = 16


def draw_lengths(key, part):
    key = jax.random.fold_in(key, 11)
    first_key, second_key, third_key = jax.random.split(key, 3)
    drawn = jax.random.randint(first_key, (IMAGES,), LEN // 8, LEN + 1, dtype=jnp.int32)
    chosen = jax.random.randint(second_key, (IMAGES // IMGS,), 0, IMGS, dtype=jnp.int32)
    longest = LEN - jax.random.randint(third_key, (IMAGES // IMGS,), 0, LEN // 16 + 1, dtype=jnp.int32)
    longest = jnp.where(jnp.arange(IMAGES // IMGS, dtype=jnp.int32) == 0, LEN, longest)
    position = jnp.arange(IMAGES, dtype=jnp.int32) % IMGS
    picked = position == jnp.repeat(chosen, IMGS)
    return jnp.where(picked, jnp.repeat(longest, IMGS), drawn).astype(jnp.int32)


def with_spikes(array, rng, source, target, shards_of, factor):
    def block_of(dim):
        return (jnp.arange(array.shape[dim]) // (array.shape[dim] // shards_of)).reshape((-1,) + (1,) * (array.ndim - 1 - dim))

    first = jax.random.permutation(rng, shards_of)[block_of(target)]
    second = (block_of(target) + shards_of // 2) % shards_of
    return jnp.where((block_of(source) == first) | (block_of(source) == second), factor * array, array)


def block_scale(rng, extent, cuts, least, largest):
    gain, own = 1.0, jax.random.fold_in(rng, 6)
    for dim, shards_of in cuts:
        heights = jnp.exp(jax.random.uniform(jax.random.fold_in(own, dim), (shards_of,), jnp.float32, least / len(cuts), largest / len(cuts)))
        gain = gain * jnp.repeat(heights, extent[dim] // shards_of).reshape([-1 if axis == dim else 1 for axis in range(len(extent))])
    return gain


def normal_values(key, dims, spread, reach, shards=(), held_as=jnp.bfloat16):
    values = spread * jax.random.normal(key, dims, jnp.float32)
    if shards:
        values = values * block_scale(key, dims, shards, -0.22, 0.18)
    return jnp.clip(values, -reach, reach).astype(held_as)


def bell_draw_with(stream_key, extent, deviation, bound, cuts, heavy, kind=jnp.bfloat16):
    array = deviation * jax.random.normal(stream_key, extent, jnp.float32)
    if cuts:
        array = array * block_scale(stream_key, extent, cuts, -0.22, 0.18)
    return jnp.clip(with_spikes(array, jax.random.fold_in(stream_key, 3), *heavy), -bound, bound).astype(kind)


def setup_inputs(seed: int = 0) -> dict:
    splits = jax.random.split(jax.random.key(seed), 17)
    return {
        "tokens": normal_values(splits[0], (IMAGES, LEN, D), 1.0, 6.0, ((0, 16), (1, 2))),
        "lengths": draw_lengths(jax.random.fold_in(splits[16], 71), 0),
        "cotangent": bell_draw_with(splits[2], (IMAGES, LEN, D), 1.0, 6.0, ((0, 16), (1, 2)), (0, 2, 16, 2.0)),
        "attn_gain": jnp.clip(1.0 + 0.15 * jax.random.normal(splits[3], (D,), jnp.float32), 0.25, 1.75),
        "attn_shift": normal_values(splits[4], (D,), 0.3, 2.0, (), jnp.float32),
        "qkv_weight": normal_values(splits[5], (D, 3 * D), D ** -0.5, 0.1875, ((0, 16),)),
        "query_bias": normal_values(splits[6], (D,), 0.5, 3.0, (), jnp.float32),
        "value_bias": normal_values(splits[7], (D,), 0.5, 3.0, (), jnp.float32),
        "out_weight": normal_values(splits[8], (D, D), (max(1, D * 4 // LEN)) ** -0.5, 3.0, ((0, 16),)),
        "out_bias": normal_values(splits[9], (D,), 0.3, 2.0, (), jnp.float32),
        "mlp_gain": jnp.clip(1.0 + 0.15 * jax.random.normal(splits[10], (D,), jnp.float32), 0.25, 1.75),
        "mlp_shift": normal_values(splits[11], (D,), 0.3, 2.0, (), jnp.float32),
        "up_weight": normal_values(splits[12], (D, FF), D ** -0.5, 0.1875, ((0, 16),)),
        "up_bias": normal_values(splits[13], (FF,), 0.5, 3.0, (), jnp.float32),
        "down_weight": normal_values(splits[14], (FF, D), FF ** -0.5, 0.09375, ((1, 16),)),
        "down_bias": normal_values(splits[15], (D,), 0.3, 2.0, (), jnp.float32),
    }


epsilon = 1e-06
masked_score = -1e+30
highest = lax.Precision.HIGHEST

@jax.custom_vjp
def low(v):
    return lax.optimization_barrier(v.astype(jnp.bfloat16)).astype(jnp.float32)

@jax.custom_vjp
def low_back(v):
    return v

def low_keep(v):
    return (low(v), None)

def low_pass(kept, grad):
    return (grad,)

def back_keep(v):
    return (v, None)

def back_low(kept, grad):
    return (low(grad),)
low.defvjp(low_keep, low_pass)
low_back.defvjp(back_keep, back_low)

def norm_layer(tensor, gain_vec, shift_vec):
    centered = tensor - lax.optimization_barrier(jnp.mean(tensor, axis=-1, keepdims=True))
    variance = lax.optimization_barrier(jnp.mean(centered * centered, axis=-1, keepdims=True))
    return centered * lax.rsqrt(variance + epsilon) * gain_vec + shift_vec

def gelu_tanh(tensor):
    return 0.5 * tensor * (1.0 + jnp.tanh(0.7978845608028654 * (tensor + 0.044715 * tensor * tensor * tensor)))

def attend(queries, keys_all, values_all, valid_keys):
    block_rows = min(512, LEN)
    query_blocks = queries.reshape(LEN // block_rows, block_rows, HEADS, HD)

    def one_block(query_block):
        raw_scores = jnp.einsum('bhd,jhd->hbj', query_block, keys_all, precision=highest)
        scores = low_back(raw_scores * HD ** (-0.5))
        scores = jnp.where(valid_keys[None, None, :], scores, masked_score)
        row_peak = lax.optimization_barrier(jnp.max(scores, axis=-1, keepdims=True))
        exponent = jnp.exp(scores - row_peak)
        weights = low(exponent / lax.optimization_barrier(jnp.sum(exponent, axis=-1, keepdims=True)))
        return jnp.einsum('hbj,jhd->bhd', weights, values_all, precision=highest)
    attended = lax.map(jax.checkpoint(one_block), query_blocks)
    return attended.reshape(LEN, HEADS * HD)

def layer(inputs, valid_keys, params):
    attn_gain, attn_shift, qkv_weight, query_bias, value_bias, out_weight, out_bias, mlp_gain, mlp_shift, up_weight, up_bias, down_weight, down_bias = params
    normed_one = low(norm_layer(inputs, attn_gain, attn_shift))
    projected = jnp.dot(normed_one, qkv_weight, precision=highest)
    queries = low(low_back(projected[:, :D] + query_bias))
    keys_all = low(low_back(projected[:, D:2 * D]))
    values_all = low(low_back(projected[:, 2 * D:] + value_bias))
    attended = attend(queries.reshape(LEN, HEADS, HD), keys_all.reshape(LEN, HEADS, HD), values_all.reshape(LEN, HEADS, HD), valid_keys)
    attended = low(low_back(attended))
    resid_one = inputs + low_back(jnp.dot(attended, out_weight, precision=highest) + out_bias)
    normed_two = low(norm_layer(resid_one, mlp_gain, mlp_shift))
    hidden = low_back(jnp.dot(normed_two, up_weight, precision=highest) + up_bias)
    active = low(gelu_tanh(hidden))
    return resid_one + low_back(jnp.dot(active, down_weight, precision=highest) + down_bias)

def reference(tokens, lengths, cotangent, attn_gain, attn_shift, qkv_weight, query_bias, value_bias, out_weight, out_bias, mlp_gain, mlp_shift, up_weight, up_bias, down_weight, down_bias):
    params = (attn_gain.astype(jnp.float32), attn_shift.astype(jnp.float32), qkv_weight.astype(jnp.float32), query_bias.astype(jnp.float32), value_bias.astype(jnp.float32), out_weight.astype(jnp.float32), out_bias.astype(jnp.float32), mlp_gain.astype(jnp.float32), mlp_shift.astype(jnp.float32), up_weight.astype(jnp.float32), up_bias.astype(jnp.float32), down_weight.astype(jnp.float32), down_bias.astype(jnp.float32))
    positions = jnp.arange(LEN, dtype=jnp.int32)
    zero_grads = tuple((jnp.zeros_like(member) for member in params))

    def per_image(totals, slices):
        image_rows, length_one, back_grad = slices
        valid_keys = positions < length_one

        def forward(inputs, weights_all):
            return layer(inputs, valid_keys, weights_all)
        result, pullback = jax.vjp(forward, image_rows, params)
        grad_image, grad_params = pullback(back_grad)
        totals = tuple((summed + added for summed, added in zip(totals, grad_params)))
        return (totals, (result.astype(jnp.bfloat16), grad_image))
    totals, (outputs, grad_tokens) = lax.scan(per_image, zero_grads, (tokens.astype(jnp.float32), lengths, cotangent.astype(jnp.float32)))
    return (outputs, grad_tokens, totals[0], totals[1], totals[2], totals[3], totals[4], totals[5], totals[6], totals[7], totals[8], totals[9], totals[10], totals[11], totals[12])
```

```python
import functools

import jax
import jax.numpy as jnp
from jax import lax
from jax.experimental import pallas as pl
from jax.experimental.pallas import tpu as pltpu
from jax.sharding import PartitionSpec as P

HD = 72
WIDE = 128
SCALE = HD ** (-0.5)
masked_score = -1e30
epsilon = 1e-06
f32, bf16 = jnp.float32, jnp.bfloat16


def spread_heads(source, target, heads):
    for head in range(heads):
        target[head, :, :HD] = source[0, :, head * HD : (head + 1) * HD]


def turn_heads(source, target, heads):
    for head in range(heads):
        target[head] = jnp.transpose(source[head])


def join_heads(source, heads):
    return jnp.concatenate([source[head, :, :HD] for head in range(heads)], axis=1)


def nt(left, right):
    return lax.dot_general(left, right, (((1,), (1,)), ((), ())), preferred_element_type=f32)


def nn(left, right):
    return jnp.dot(left, right, preferred_element_type=f32)


def attend_kernel(parts, heads, block, earlier, info, *refs):
    q_in = refs[0]
    k_in = refs[1 : 1 + parts]
    v_in = refs[1 + parts : 1 + 2 * parts]
    refs = refs[1 + 2 * parts + earlier :]
    out, lse = refs[:2]
    scratch = refs[2:]
    q_s, o_s = scratch[:2]
    k_s = scratch[2 : 2 + parts]
    vt_s = scratch[2 + parts : 2 + 2 * parts]
    head = pl.program_id(0)
    rows = q_s.shape[1]

    @pl.when(head == 0)
    def _():
        q_s[...] = jnp.zeros_like(q_s)
        spread_heads(q_in, q_s, heads)
        for part in range(parts):
            k_s[part][...] = jnp.zeros_like(k_s[part])
            spread_heads(v_in[part], k_s[part], heads)
            turn_heads(k_s[part], vt_s[part], heads)
            spread_heads(k_in[part], k_s[part], heads)

    masks = []
    for part in range(parts):
        length = k_s[part].shape[1]
        masks.append(
            info[1 + part] + lax.broadcasted_iota(jnp.int32, (length, 1), 0) < info[0]
        )
    for start in range(0, rows, block):
        q_rows = q_s[head, start : start + block]
        scores = [
            jnp.where(masks[part], nt(k_s[part][head], q_rows), masked_score)
            for part in range(parts)
        ]
        peak = functools.reduce(
            jnp.maximum, [jnp.max(member, axis=0, keepdims=True) for member in scores]
        )
        total = 0.0
        result = 0.0
        for part in range(parts):
            grown = jnp.exp((scores[part] - peak) * SCALE)
            total = total + jnp.sum(grown, axis=0, keepdims=True)
            result = result + nn(vt_s[part][head], grown.astype(bf16))
        result = result / total
        o_s[head, start : start + block] = jnp.transpose(result).astype(bf16)
        lse[0, :, start : start + block] = peak * SCALE + jnp.log(total)

    @pl.when(head == heads - 1)
    def _():
        out[0] = join_heads(o_s, heads)


def attend_back_kernel(parts, heads, block, earlier, info, *refs):
    q_in, d_in, lse = refs[:3]
    k_in = refs[3 : 3 + parts]
    v_in = refs[3 + parts : 3 + 2 * parts]
    refs = refs[3 + 2 * parts + earlier :]
    dq_out = refs[0]
    dk_out = refs[1 : 1 + parts]
    dv_out = refs[1 + parts : 1 + 2 * parts]
    refs = refs[1 + 2 * parts :]
    q_s, d_s, dq_s = refs[:3]
    refs = refs[3:]
    k_s, v_s, kt_s, dk_s, dv_s = (refs[i * parts : (i + 1) * parts] for i in range(5))
    head = pl.program_id(0)
    rows = q_s.shape[1]

    @pl.when(head == 0)
    def _():
        q_s[...] = jnp.zeros_like(q_s)
        d_s[...] = jnp.zeros_like(d_s)
        spread_heads(q_in, q_s, heads)
        spread_heads(d_in, d_s, heads)
        for part in range(parts):
            k_s[part][...] = jnp.zeros_like(k_s[part])
            v_s[part][...] = jnp.zeros_like(v_s[part])
            spread_heads(k_in[part], k_s[part], heads)
            spread_heads(v_in[part], v_s[part], heads)
            turn_heads(k_s[part], kt_s[part], heads)

    masks = []
    for part in range(parts):
        length = k_s[part].shape[1]
        masks.append(
            info[1 + part] + lax.broadcasted_iota(jnp.int32, (length, 1), 0) < info[0]
        )
    d_key = [0.0] * parts
    d_value = [0.0] * parts
    for start in range(0, rows, block):
        q_rows = q_s[head, start : start + block]
        d_rows = d_s[head, start : start + block]
        level = lse[0, :, start : start + block]
        probs = []
        d_probs = []
        row_dot = 0.0
        for part in range(parts):
            scores = jnp.where(masks[part], nt(k_s[part][head], q_rows) * SCALE, masked_score)
            probs.append(jnp.exp(scores - level))
            d_probs.append(nt(v_s[part][head], d_rows))
            row_dot = row_dot + jnp.sum(probs[part] * d_probs[part], axis=0, keepdims=True)
        d_query = 0.0
        for part in range(parts):
            d_scores = (probs[part] * (d_probs[part] - row_dot)).astype(bf16)
            d_value[part] = d_value[part] + nn(probs[part].astype(bf16), d_rows)
            d_key[part] = d_key[part] + nn(d_scores, q_rows)
            d_query = d_query + nn(kt_s[part][head], d_scores)
        dq_s[head, start : start + block] = jnp.transpose(d_query * SCALE).astype(bf16)
    for part in range(parts):
        dk_s[part][head] = (d_key[part] * SCALE).astype(bf16)
        dv_s[part][head] = d_value[part].astype(bf16)

    @pl.when(head == heads - 1)
    def _():
        dq_out[0] = join_heads(dq_s, heads)
        for part in range(parts):
            dk_out[part][0] = join_heads(dk_s[part], heads)
            dv_out[part][0] = join_heads(dv_s[part], heads)


def whole(shape):
    return pl.BlockSpec(shape, lambda head: (0,) * len(shape))


def anywhere(arrays):
    return [pl.BlockSpec(memory_space=pl.ANY)] * len(arrays)


def attend(info, query, keys, values, earlier=(), block=512):
    _, rows, width = query.shape
    heads = width // HD
    parts = len(keys)
    lengths = [member.shape[1] for member in keys]
    total = sum(lengths)
    return pl.pallas_call(
        functools.partial(attend_kernel, parts, heads, min(block, rows), len(earlier)),
        grid=(heads,),
        in_specs=[pl.BlockSpec(memory_space=pltpu.SMEM), whole(query.shape)]
        + [whole(member.shape) for member in (*keys, *values)]
        + anywhere(earlier),
        out_specs=[whole(query.shape), pl.BlockSpec((1, 1, rows), lambda head: (head, 0, 0))],
        out_shape=[
            jax.ShapeDtypeStruct(query.shape, bf16),
            jax.ShapeDtypeStruct((heads, 1, rows), f32),
        ],
        scratch_shapes=[pltpu.VMEM((heads, rows, WIDE), bf16)] * 2
        + [pltpu.VMEM((heads, length, WIDE), bf16) for length in lengths]
        + [pltpu.VMEM((heads, WIDE, length), bf16) for length in lengths],
        compiler_params=pltpu.CompilerParams(vmem_limit_bytes=48 * 1024 * 1024),
        cost_estimate=pl.CostEstimate(
            flops=4 * heads * rows * total * 256,
            bytes_accessed=4 * (rows + total) * width,
            transcendentals=heads * rows * total,
        ),
    )(info, query, *keys, *values, *earlier)


def attend_back(info, query, d_out, lse, keys, values, earlier=(), block=256):
    _, rows, width = query.shape
    heads = width // HD
    parts = len(keys)
    lengths = [member.shape[1] for member in keys]
    total = sum(lengths)
    results = pl.pallas_call(
        functools.partial(attend_back_kernel, parts, heads, min(block, rows), len(earlier)),
        grid=(heads,),
        in_specs=[
            pl.BlockSpec(memory_space=pltpu.SMEM),
            whole(query.shape),
            whole(query.shape),
            pl.BlockSpec((1, 1, rows), lambda head: (head, 0, 0)),
        ]
        + [whole(member.shape) for member in (*keys, *values)]
        + anywhere(earlier),
        out_specs=[whole(member.shape) for member in (query, *keys, *values)],
        out_shape=[
            jax.ShapeDtypeStruct(member.shape, bf16) for member in (query, *keys, *values)
        ],
        scratch_shapes=[pltpu.VMEM((heads, rows, WIDE), bf16)] * 3
        + [pltpu.VMEM((heads, length, WIDE), bf16) for length in lengths] * 2
        + [pltpu.VMEM((heads, WIDE, length), bf16) for length in lengths]
        + [pltpu.VMEM((heads, length, WIDE), bf16) for length in lengths] * 2,
        compiler_params=pltpu.CompilerParams(vmem_limit_bytes=56 * 1024 * 1024),
        cost_estimate=pl.CostEstimate(
            flops=10 * heads * rows * total * 256,
            bytes_accessed=8 * (rows + total) * width,
            transcendentals=heads * rows * total,
        ),
    )(info, query, d_out, lse, *keys, *values, *earlier)
    return results[0], results[1 : 1 + parts], results[1 + parts :]


def contract_rows(left_rows, right_rows):
    return lax.dot_general(
        left_rows, right_rows, (((0,), (0,)), ((), ())), preferred_element_type=f32
    )


def column_sum(tensor):
    return jnp.sum(tensor.astype(f32), axis=0)


def after(value, *earlier):
    return lax.optimization_barrier((value, *earlier))[0]


def norm_parts(tensor):
    centered = tensor - jnp.mean(tensor, axis=-1, keepdims=True)
    scale = lax.rsqrt(jnp.mean(centered * centered, axis=-1, keepdims=True) + epsilon)
    return centered * scale, scale


def norm_back(upstream, normal, scale, gain):
    weighted = upstream * gain
    mean_one = jnp.mean(weighted, axis=-1, keepdims=True)
    mean_two = jnp.mean(weighted * normal, axis=-1, keepdims=True)
    return scale * (weighted - mean_one - normal * mean_two)


def gelu_and_slope(tensor):
    square = tensor * tensor
    bent = jnp.tanh(0.7978845608028654 * tensor * (1.0 + 0.044715 * square))
    half = 0.5 * (1.0 + bent)
    slope = half + 0.5 * tensor * (1.0 - bent * bent) * 0.7978845608028654 * (
        1.0 + 0.134145 * square
    )
    return tensor * half, slope


def place_kernel(count, slots, *refs):
    pieces, (out, sems) = refs[:count], refs[-2:]
    copies = []
    for piece in pieces:
        for line in range(piece.shape[0]):
            for part in range(piece.shape[1]):
                index = len(copies)
                copies.append(
                    pltpu.make_async_copy(
                        piece.at[line, part], out.at[slots[index]], sems.at[index]
                    )
                )
    for copy in copies:
        copy.start()
    for copy in copies:
        copy.wait()


def place(pieces, slots, earlier=()):
    rows, columns = pieces[0].shape[2:]
    total = sum(piece.shape[0] * piece.shape[1] for piece in pieces)
    return pl.pallas_call(
        functools.partial(place_kernel, len(pieces)),
        in_specs=[pl.BlockSpec(memory_space=pltpu.SMEM)]
        + anywhere(pieces)
        + anywhere(earlier),
        out_specs=pl.BlockSpec(memory_space=pltpu.VMEM),
        out_shape=jax.ShapeDtypeStruct((total, rows, columns), pieces[0].dtype),
        scratch_shapes=[pltpu.SemaphoreType.DMA((total,))],
        compiler_params=pltpu.CompilerParams(vmem_limit_bytes=32 * 1024 * 1024),
        cost_estimate=pl.CostEstimate(
            flops=0, bytes_accessed=4 * total * rows * columns, transcendentals=0
        ),
    )(slots, *pieces, *earlier)


class Grid:
    def __init__(self, shard_rows):
        self.size = lax.axis_size("fsdp")
        self.apart = HD // shard_rows
        self.depth = self.size // 4
        me = lax.axis_index("fsdp")
        self.twin = (me // self.apart) % 2
        member = (me // (2 * self.apart)) * self.apart + me % self.apart
        self.z, self.x = member // 2, member % 2

    def index(self, z, x, twin):
        member = z * 2 + x
        return (
            (member // self.apart) * 2 * self.apart + twin * self.apart + member % self.apart
        )

    def pairs(self, step_z=0, step_x=0, step_twin=0):
        return [
            (
                self.index(z, x, twin),
                self.index((z + step_z) % self.depth, x ^ step_x, twin ^ step_twin),
            )
            for z in range(self.depth)
            for x in range(2)
            for twin in range(2)
        ]

    def send(self, value, **steps):
        return lax.ppermute(value, "fsdp", self.pairs(**steps))

    def members(self):
        return [
            ((self.z + step_z) % self.depth) * 2 + (self.x ^ step_x)
            for step_x in range(2)
            for step_z in range(self.depth)
        ]

    def shards(self):
        return [
            (member // self.apart) * 2 * self.apart
            + (self.twin ^ step) * self.apart
            + member % self.apart
            for member in self.members()
            for step in range(2)
        ]

    def shards_by_seq(self):
        mine = self.shards()
        first = lax.axis_index("seq") == 0
        kinds = [mine[0::2], mine[1::2]]
        return [jnp.where(first, one, two) for one, two in zip(*kinds)] + [
            jnp.where(first, two, one) for one, two in zip(*kinds)
        ]

    def groups(self):
        return [
            [self.index(member // 2, member % 2, twin) for member in range(2 * self.depth)]
            for twin in range(2)
        ]

    def gather(self, block):
        whole = lax.all_gather(block, "fsdp", axis_index_groups=self.groups())
        _, _, rows, columns = whole.shape
        whole = whole.reshape(-1, self.apart, 2, rows, columns).transpose(0, 2, 1, 3, 4)
        return whole.reshape(-1, columns)

    def scatter(self, matrix):
        columns = matrix.shape[1]
        matrix = matrix.reshape(2 * self.depth // self.apart, 2, self.apart, -1, columns)
        matrix = matrix.transpose(0, 2, 1, 3, 4).reshape(-1, columns)
        return lax.psum_scatter(
            matrix, "fsdp", scatter_dimension=0, axis_index_groups=self.groups(), tiled=True
        )

    def own_half(self, halves):
        return jnp.where(self.twin == 0, halves[0], halves[1])

    def other_half(self, halves):
        return jnp.where(self.twin == 0, halves[1], halves[0])

    def swap_rows(self, partial, rows):
        sent = jnp.concatenate([partial[rows:], partial[:rows]], axis=0).astype(bf16)
        return self.send(sent, step_twin=1).astype(f32)

    def swap_mine(self, first, second):
        mine, sent = self.in_order(first, second)
        return self.in_order(mine, self.send(sent.astype(bf16), step_twin=1).astype(f32))

    def in_order(self, mine, other):
        first = self.twin == 0
        return jnp.where(first, mine, other), jnp.where(first, other, mine)


def order_matrix(places, rows):
    count = len(places) * rows
    source = (jnp.stack(places) * rows)[:, None] + jnp.arange(rows, dtype=jnp.int32)[None, :]
    return (jnp.arange(count, dtype=jnp.int32)[:, None] == source.reshape(1, count)).astype(bf16)


def reorder(rows, matrix):
    return jnp.dot(rows, matrix, preferred_element_type=f32).astype(bf16)


def gather_z(grid, block):
    sent = {step: grid.send(block, step_z=step) for step in range(1, grid.depth)}
    return [block] + [sent[grid.depth - step] for step in range(1, grid.depth)]


def gather_x(grid, blocks):
    joined = jnp.stack(blocks)
    return joined, grid.send(joined, step_x=1)


def gather_all(grid, block):
    lines = gather_z(grid, block)
    return lines, list(gather_x(grid, lines))


def by_seq(first_value, second_value):
    return jnp.where(lax.axis_index("seq") == 0, first_value, second_value)


def gather_by_seq(grid, block):
    lines = gather_z(grid, by_seq(block[:1], block[1:]))
    joined, across = gather_x(grid, lines)
    return lines, [joined, across, swap_seq(joined), swap_seq(across)]


def halves_of(left, right):
    half = left.shape[1] // 2
    going = contract_rows(left[:, half:], right).astype(bf16)
    return contract_rows(left[:, :half], right).astype(bf16), going


def add_pieces(kept, came, count):
    rows = kept.shape[0] // count
    return [
        (
            kept[step * rows : (step + 1) * rows].astype(f32)
            + came[step * rows : (step + 1) * rows].astype(f32)
        ).astype(bf16)
        for step in range(count)
    ]


def swap_seq(value):
    return lax.ppermute(value, "seq", [(0, 1), (1, 0)])


def sum_z(grid, sums):
    total = sums[0].astype(f32)
    for step in range(1, grid.depth):
        total = total + grid.send(sums[step], step_z=step).astype(f32)
    return total.astype(bf16)


class ScatterX:
    def __init__(self, grid, left, right):
        self.grid = grid
        self.kept, self.going = halves_of(left, right)
        self.came = grid.send(self.going, step_x=1)

    def add(self):
        self.sums = add_pieces(self.kept, self.came, self.grid.depth)
        return self.sums

    def finish(self):
        return sum_seq(sum_z(self.grid, self.sums))


class ScatterY:
    def __init__(self, grid, left, right):
        self.grid = grid
        self.kept, self.going = halves_of(left, right)
        self.came = swap_seq(self.going)

    def cross(self):
        self.kept, self.going = add_pieces(self.kept, self.came, 2)
        self.came = self.grid.send(self.going, step_x=1)
        return [self.kept, self.going]

    def add(self):
        self.sums = add_pieces(self.kept, self.came, self.grid.depth)
        return self.sums

    def finish(self):
        total = sum_z(self.grid, self.sums)
        other = swap_seq(total)
        first = lax.axis_index("seq") == 0
        return jnp.concatenate(
            [jnp.where(first, total, other), jnp.where(first, other, total)], axis=0
        ).astype(f32)


def sum_seq(value):
    groups = lax.axis_size("seq")
    if groups == 2:
        return value.astype(f32) + lax.ppermute(value, "seq", [(0, 1), (1, 0)]).astype(f32)
    return lax.psum(value.astype(f32), "seq")


def swap_twin(grid, total):
    rows = total.shape[0] // 2
    other = grid.send(total[rows:].astype(bf16), step_twin=1).astype(f32)
    return grid.in_order(total[:rows], other)


def sum_all(vector):
    for axis in ("fsdp", "seq"):
        count = lax.axis_size(axis)
        step = 1
        while step < count:
            vector = vector + lax.ppermute(
                vector, axis, [(member, member ^ step) for member in range(count)]
            )
            step *= 2
    return vector


def body(
    tokens,
    lengths,
    cotangent,
    attn_gain,
    attn_shift,
    qkv_weight,
    query_bias,
    value_bias,
    out_weight,
    out_bias,
    mlp_gain,
    mlp_shift,
    up_weight,
    up_bias,
    down_weight,
    down_bias,
):
    groups = lax.axis_size("seq")
    images, local_len, width = tokens.shape
    shard_rows = qkv_weight.shape[0]
    hidden_half = up_weight.shape[1] // 2
    rows = images * local_len
    heads = width // HD
    own_width = width // 2
    grid = Grid(shard_rows)
    all_members = jnp.stack(grid.members())

    def by_kind(matrix):
        lead = matrix.shape[0]
        split = matrix.reshape(lead, -1, heads // 2, 2, HD)
        return [split[:, :, :, kind].reshape(lead, -1) for kind in range(2)]

    def vector_kind(vector):
        return grid.own_half([vector.reshape(-1, 2, HD)[:, kind].reshape(-1) for kind in range(2)])

    def two_halves(matrix):
        return [matrix[:, :hidden_half], matrix[:, hidden_half:]]

    def pair_up(halves):
        other = grid.send(grid.other_half(halves), step_twin=1)
        return jnp.stack([grid.own_half(halves), other])

    qkv_block = pair_up(by_kind(qkv_weight))
    pair_block = qkv_block[:, :, own_width:]
    all_kinds = jnp.stack(grid.shards())
    up_block = pair_up(two_halves(up_weight))
    down_block = pair_up(two_halves(down_weight.T))
    own_up = grid.gather(jnp.stack(grid.in_order(*up_block)))
    own_down = grid.gather(jnp.stack(grid.in_order(*down_block)))
    if groups == 2:
        pair_lines, pair_pieces = gather_by_seq(grid, pair_block)
        pair_slots = jnp.stack(grid.shards_by_seq())
    else:
        pair_lines, pair_pieces = gather_all(grid, pair_block)
        pair_slots = all_kinds
    query_lines, query_pieces = gather_all(
        grid, after(qkv_block[:, :, :own_width], pair_lines[-1])
    )
    out_lines, out_pieces = gather_all(grid, after(out_weight[None], query_lines[-1]))

    def both(value):
        flat = value.reshape(rows, width)
        return jnp.concatenate([flat, grid.send(flat, step_twin=1)], axis=0)

    inputs = both(tokens).astype(f32)
    back_low = both(cotangent)
    sizes = jnp.concatenate([lengths, grid.send(lengths, step_twin=1)])

    order = order_matrix(grid.shards(), shard_rows)
    if groups == 2:
        scatter_seq, seq_order = ScatterY, order_matrix(grid.shards_by_seq(), shard_rows)
    else:
        scatter_seq, seq_order = ScatterX, order
    own_order = order_matrix(grid.members(), shard_rows)

    normal_one, scale_one = norm_parts(inputs)
    normed_one = (normal_one * attn_gain + attn_shift).astype(bf16)
    own_pair = place(pair_pieces, pair_slots, query_lines[1:]).reshape(width, 2 * own_width)
    pair_bias = jnp.concatenate([jnp.zeros((own_width,), f32), vector_kind(value_bias)])
    pairs = (jnp.dot(normed_one, own_pair, preferred_element_type=f32) + pair_bias).astype(bf16)
    own_query = place(query_pieces, all_kinds, out_lines[1:])
    own_query = own_query.reshape(width, own_width)
    queries = (
        jnp.dot(normed_one, own_query, preferred_element_type=f32) + vector_kind(query_bias)
    ).astype(bf16)

    place_seq = lax.axis_index("seq") * local_len
    attended_parts, saved = [], []
    for image in range(2 * images):
        span = slice(image * local_len, (image + 1) * local_len)
        query, near = queries[span][None], pairs[span][None]
        key, value = near[:, :, :own_width], near[:, :, own_width:]
        if groups == 2:
            far = swap_seq(near)
            key_parts = (key, far[:, :, :own_width])
            value_parts = (value, far[:, :, own_width:])
            info = jnp.stack([sizes[image], place_seq, local_len - place_seq])
        else:
            key_parts = (lax.all_gather(key, "seq", axis=1, tiled=True),)
            value_parts = (lax.all_gather(value, "seq", axis=1, tiled=True),)
            info = jnp.stack([sizes[image], jnp.zeros_like(sizes[image])])
        attended_part, lse = attend(info, query, key_parts, value_parts)
        attended_parts.append(attended_part[0])
        saved.append((info, query, key_parts, value_parts, lse))
    attended = jnp.concatenate(attended_parts, axis=0)

    own_out = place(out_pieces, all_members)
    own_out = own_out.reshape(own_width, width)
    partial = jnp.dot(attended, own_out, preferred_element_type=f32)
    resid = inputs + partial + grid.swap_rows(partial, rows) + out_bias
    normal_two, scale_two = norm_parts(resid)
    normed_two = (normal_two * mlp_gain + mlp_shift).astype(bf16)
    own_up_bias = grid.own_half([up_bias[:hidden_half], up_bias[hidden_half:]])
    hidden = jnp.dot(normed_two, own_up, preferred_element_type=f32) + own_up_bias
    active, slope = gelu_and_slope(hidden)
    active, slope = lax.optimization_barrier((active.astype(bf16), slope.astype(bf16)))
    grad_down = contract_rows(back_low, active).astype(bf16)
    back_low, grad_down = lax.optimization_barrier((back_low, grad_down))
    grad_down = grid.scatter(grad_down)

    d_active = jnp.dot(back_low, own_down, preferred_element_type=f32)
    d_hidden = (d_active * slope).astype(bf16)
    grad_up = contract_rows(normed_two, d_hidden).astype(bf16)
    d_hidden, grad_up = lax.optimization_barrier((d_hidden, grad_up))
    grad_up = grid.scatter(grad_up)
    partial = lax.dot_general(
        d_hidden, own_up, (((1,), (1,)), ((), ())), preferred_element_type=f32
    )
    d_two = partial + grid.swap_rows(partial, rows)
    d_resid = back_low.astype(f32) + norm_back(d_two, normal_two, scale_two, mlp_gain)
    out_low = d_resid.astype(bf16)
    grad_out = ScatterX(grid, reorder(attended, own_order), out_low)
    d_attended = lax.dot_general(
        out_low, own_out, (((1,), (1,)), ((), ())), preferred_element_type=f32
    ).astype(bf16)

    d_query, d_key, d_value = [], [], []
    for image in range(2 * images):
        span = slice(image * local_len, (image + 1) * local_len)
        info, query, key_parts, value_parts, lse = saved[image]
        if image == 0:
            on_their_way = [grad_out.kept, grad_out.going]
        else:
            on_their_way = grad_out.add() if image == images else []
        d_query_part, key_grads, value_grads = attend_back(
            info,
            query,
            d_attended[span][None],
            lse,
            key_parts,
            value_parts,
            on_their_way,
        )
        d_query.append(d_query_part[0])
        if groups == 2:
            far = swap_seq(jnp.concatenate([key_grads[1], value_grads[1]], axis=2))
            d_key.append((key_grads[0], far[:, :, :own_width]))
            d_value.append((value_grads[0], far[:, :, own_width:]))
        else:
            for into, member in ((d_key, key_grads[0]), (d_value, value_grads[0])):
                into.append(
                    (
                        lax.psum_scatter(
                            member.astype(f32), "seq", scatter_dimension=1, tiled=True
                        ),
                    )
                )
    d_query = jnp.concatenate(d_query, axis=0)
    one_rows = reorder(normed_one, order)
    grad_query = ScatterX(grid, one_rows, d_query)
    late_active, grad_query.kept = lax.optimization_barrier((active, grad_query.kept))
    partial = lax.dot_general(
        late_active, own_down, (((1,), (1,)), ((), ())), preferred_element_type=f32
    )
    came = grid.send(partial[rows:].astype(bf16), step_twin=1).astype(f32)
    outputs = (resid[:rows] + partial[:rows] + came + down_bias).astype(bf16)

    d_key, d_value = (
        jnp.concatenate(
            [sum(part.astype(f32) for part in parts)[0].astype(bf16) for parts in member], axis=0
        )
        for member in (d_key, d_value)
    )
    grad_key = scatter_seq(grid, reorder(normed_one, seq_order), d_key)
    grad_value = ScatterX(grid, one_rows, d_value)
    partial = sum(
        lax.dot_general(member, weight, (((1,), (1,)), ((), ())), preferred_element_type=f32)
        for member, weight in (
            (d_query, own_query),
            (d_key, own_pair[:, :own_width]),
            (d_value, own_pair[:, own_width:]),
        )
    )
    d_one = partial[:rows] + grid.send(partial[rows:].astype(bf16), step_twin=1).astype(f32)
    grad_tokens = d_resid[:rows] + norm_back(d_one, normal_one[:rows], scale_one[:rows], attn_gain)
    grad_query.add()
    if groups == 2:
        grad_key.cross()
    grad_value.add()
    grad_key.add()
    grad_out = grad_out.finish()
    grad_up, grad_down = sum_seq(grad_up), sum_seq(grad_down)
    grad_qkv = jnp.concatenate(
        [grad_query.finish(), grad_key.finish(), grad_value.finish()], axis=1
    )

    def by_kinds(total):
        half = total.shape[0] // 2
        return jnp.concatenate(grid.swap_mine(total[:half], total[half:]), axis=1)

    grad_up, grad_down = by_kinds(grad_up), by_kinds(grad_down).T
    grad_qkv = jnp.stack(
        [member.reshape(shard_rows, 3, heads // 2, HD) for member in swap_twin(grid, grad_qkv)],
        axis=3,
    ).reshape(shard_rows, 3 * width)

    def at_kind(vector, shape, axis):
        vector = vector.reshape(shape)
        nothing = jnp.zeros_like(vector)
        return jnp.stack(grid.in_order(vector, nothing), axis=axis).reshape(-1)

    vectors = sum_all(
        jnp.concatenate(
            [
                column_sum(d_one * normal_one[:rows]),
                column_sum(d_one),
                at_kind(column_sum(d_query), (heads // 2, HD), 1),
                at_kind(column_sum(d_value), (heads // 2, HD), 1),
                column_sum(out_low[:rows]),
                column_sum(d_two[:rows] * normal_two[:rows]),
                column_sum(d_two[:rows]),
                column_sum(back_low[:rows]),
                at_kind(column_sum(d_hidden), (-1,), 0),
            ]
        )
    )
    (
        grad_attn_gain,
        grad_attn_shift,
        grad_query_bias,
        grad_value_bias,
        grad_out_bias,
        grad_mlp_gain,
        grad_mlp_shift,
        grad_down_bias,
    ) = (vectors[step * width : (step + 1) * width] for step in range(8))
    grad_up_bias = vectors[8 * width :]
    shape = (images, local_len, width)
    return (
        outputs.reshape(shape),
        grad_tokens.reshape(shape),
        grad_attn_gain,
        grad_attn_shift,
        grad_qkv,
        grad_query_bias,
        grad_value_bias,
        grad_out,
        grad_out_bias,
        grad_mlp_gain,
        grad_mlp_shift,
        grad_up,
        grad_up_bias,
        grad_down,
        grad_down_bias,
    )


def solution(mesh):
    return jax.shard_map(
        body,
        mesh=mesh,
        in_specs=(
            P("fsdp", "seq", None),
            P("fsdp"),
            P("fsdp", "seq", None),
            P(),
            P(),
            P("fsdp", None),
            P(),
            P(),
            P("fsdp", None),
            P(),
            P(),
            P(),
            P("fsdp", None),
            P(),
            P(None, "fsdp"),
            P(),
        ),
        out_specs=(
            P("fsdp", "seq", None),
            P("fsdp", "seq", None),
            P(),
            P(),
            P("fsdp", None),
            P(),
            P(),
            P("fsdp", None),
            P(),
            P(),
            P(),
            P("fsdp", None),
            P(),
            P(None, "fsdp"),
            P(),
        ),
        check_vma=False,
    )
```

```python
import functools

import jax
import jax.numpy as jnp
from jax import lax
from jax.experimental import pallas as pl
from jax.experimental.pallas import tpu as pltpu
from jax.sharding import PartitionSpec as P

HD = 72
WIDE = 128
SCALE = HD ** (-0.5)
masked_score = -1e30
epsilon = 1e-06
f32, bf16 = jnp.float32, jnp.bfloat16


def spread_heads(source, target, heads):
    for head in range(heads):
        target[head, :, :HD] = source[0, :, head * HD : (head + 1) * HD]


def turn_heads(source, target, heads):
    for head in range(heads):
        target[head] = jnp.transpose(source[head])


def join_heads(source, heads):
    return jnp.concatenate([source[head, :, :HD] for head in range(heads)], axis=1)


def nt(left, right):
    return lax.dot_general(left, right, (((1,), (1,)), ((), ())), preferred_element_type=f32)


def nn(left, right):
    return jnp.dot(left, right, preferred_element_type=f32)


def attend_kernel(parts, heads, block, earlier, info, *refs):
    q_in = refs[0]
    k_in = refs[1 : 1 + parts]
    v_in = refs[1 + parts : 1 + 2 * parts]
    refs = refs[1 + 2 * parts + earlier :]
    out, lse = refs[:2]
    scratch = refs[2:]
    q_s, o_s = scratch[:2]
    k_s = scratch[2 : 2 + parts]
    vt_s = scratch[2 + parts : 2 + 2 * parts]
    head = pl.program_id(0)
    rows = q_s.shape[1]

    @pl.when(head == 0)
    def _():
        q_s[...] = jnp.zeros_like(q_s)
        spread_heads(q_in, q_s, heads)
        for part in range(parts):
            k_s[part][...] = jnp.zeros_like(k_s[part])
            spread_heads(v_in[part], k_s[part], heads)
            turn_heads(k_s[part], vt_s[part], heads)
            spread_heads(k_in[part], k_s[part], heads)

    masks = []
    for part in range(parts):
        length = k_s[part].shape[1]
        masks.append(
            info[1 + part] + lax.broadcasted_iota(jnp.int32, (length, 1), 0) < info[0]
        )
    for start in range(0, rows, block):
        q_rows = q_s[head, start : start + block]
        scores = [
            jnp.where(masks[part], nt(k_s[part][head], q_rows), masked_score)
            for part in range(parts)
        ]
        peak = functools.reduce(
            jnp.maximum, [jnp.max(member, axis=0, keepdims=True) for member in scores]
        )
        total = 0.0
        result = 0.0
        for part in range(parts):
            grown = jnp.exp((scores[part] - peak) * SCALE)
            total = total + jnp.sum(grown, axis=0, keepdims=True)
            result = result + nn(vt_s[part][head], grown.astype(bf16))
        result = result / total
        o_s[head, start : start + block] = jnp.transpose(result).astype(bf16)
        lse[0, :, start : start + block] = peak * SCALE + jnp.log(total)

    @pl.when(head == heads - 1)
    def _():
        out[0] = join_heads(o_s, heads)


def attend_back_kernel(parts, heads, block, earlier, info, *refs):
    q_in, d_in, lse = refs[:3]
    k_in = refs[3 : 3 + parts]
    v_in = refs[3 + parts : 3 + 2 * parts]
    refs = refs[3 + 2 * parts + earlier :]
    dq_out = refs[0]
    dk_out = refs[1 : 1 + parts]
    dv_out = refs[1 + parts : 1 + 2 * parts]
    refs = refs[1 + 2 * parts :]
    q_s, d_s, dq_s = refs[:3]
    refs = refs[3:]
    k_s, v_s, kt_s, dk_s, dv_s = (refs[i * parts : (i + 1) * parts] for i in range(5))
    head = pl.program_id(0)
    rows = q_s.shape[1]

    @pl.when(head == 0)
    def _():
        q_s[...] = jnp.zeros_like(q_s)
        d_s[...] = jnp.zeros_like(d_s)
        spread_heads(q_in, q_s, heads)
        spread_heads(d_in, d_s, heads)
        for part in range(parts):
            k_s[part][...] = jnp.zeros_like(k_s[part])
            v_s[part][...] = jnp.zeros_like(v_s[part])
            spread_heads(k_in[part], k_s[part], heads)
            spread_heads(v_in[part], v_s[part], heads)
            turn_heads(k_s[part], kt_s[part], heads)

    masks = []
    for part in range(parts):
        length = k_s[part].shape[1]
        masks.append(
            info[1 + part] + lax.broadcasted_iota(jnp.int32, (length, 1), 0) < info[0]
        )
    d_key = [0.0] * parts
    d_value = [0.0] * parts
    for start in range(0, rows, block):
        q_rows = q_s[head, start : start + block]
        d_rows = d_s[head, start : start + block]
        level = lse[0, :, start : start + block]
        probs = []
        d_probs = []
        row_dot = 0.0
        for part in range(parts):
            scores = jnp.where(masks[part], nt(k_s[part][head], q_rows) * SCALE, masked_score)
            probs.append(jnp.exp(scores - level))
            d_probs.append(nt(v_s[part][head], d_rows))
            row_dot = row_dot + jnp.sum(probs[part] * d_probs[part], axis=0, keepdims=True)
        d_query = 0.0
        for part in range(parts):
            d_scores = (probs[part] * (d_probs[part] - row_dot)).astype(bf16)
            d_value[part] = d_value[part] + nn(probs[part].astype(bf16), d_rows)
            d_key[part] = d_key[part] + nn(d_scores, q_rows)
            d_query = d_query + nn(kt_s[part][head], d_scores)
        dq_s[head, start : start + block] = jnp.transpose(d_query * SCALE).astype(bf16)
    for part in range(parts):
        dk_s[part][head] = (d_key[part] * SCALE).astype(bf16)
        dv_s[part][head] = d_value[part].astype(bf16)

    @pl.when(head == heads - 1)
    def _():
        dq_out[0] = join_heads(dq_s, heads)
        for part in range(parts):
            dk_out[part][0] = join_heads(dk_s[part], heads)
            dv_out[part][0] = join_heads(dv_s[part], heads)


def whole(shape):
    return pl.BlockSpec(shape, lambda head: (0,) * len(shape))


def anywhere(arrays):
    return [pl.BlockSpec(memory_space=pl.ANY)] * len(arrays)


def attend(info, query, keys, values, earlier=(), block=512):
    _, rows, width = query.shape
    heads = width // HD
    parts = len(keys)
    lengths = [member.shape[1] for member in keys]
    total = sum(lengths)
    return pl.pallas_call(
        functools.partial(attend_kernel, parts, heads, min(block, rows), len(earlier)),
        grid=(heads,),
        in_specs=[pl.BlockSpec(memory_space=pltpu.SMEM), whole(query.shape)]
        + [whole(member.shape) for member in (*keys, *values)]
        + anywhere(earlier),
        out_specs=[whole(query.shape), pl.BlockSpec((1, 1, rows), lambda head: (head, 0, 0))],
        out_shape=[
            jax.ShapeDtypeStruct(query.shape, bf16),
            jax.ShapeDtypeStruct((heads, 1, rows), f32),
        ],
        scratch_shapes=[pltpu.VMEM((heads, rows, WIDE), bf16)] * 2
        + [pltpu.VMEM((heads, length, WIDE), bf16) for length in lengths]
        + [pltpu.VMEM((heads, WIDE, length), bf16) for length in lengths],
        compiler_params=pltpu.CompilerParams(vmem_limit_bytes=48 * 1024 * 1024),
        cost_estimate=pl.CostEstimate(
            flops=4 * heads * rows * total * 256,
            bytes_accessed=4 * (rows + total) * width,
            transcendentals=heads * rows * total,
        ),
    )(info, query, *keys, *values, *earlier)


def attend_back(info, query, d_out, lse, keys, values, earlier=(), block=256):
    _, rows, width = query.shape
    heads = width // HD
    parts = len(keys)
    lengths = [member.shape[1] for member in keys]
    total = sum(lengths)
    results = pl.pallas_call(
        functools.partial(attend_back_kernel, parts, heads, min(block, rows), len(earlier)),
        grid=(heads,),
        in_specs=[
            pl.BlockSpec(memory_space=pltpu.SMEM),
            whole(query.shape),
            whole(query.shape),
            pl.BlockSpec((1, 1, rows), lambda head: (head, 0, 0)),
        ]
        + [whole(member.shape) for member in (*keys, *values)]
        + anywhere(earlier),
        out_specs=[whole(member.shape) for member in (query, *keys, *values)],
        out_shape=[
            jax.ShapeDtypeStruct(member.shape, bf16) for member in (query, *keys, *values)
        ],
        scratch_shapes=[pltpu.VMEM((heads, rows, WIDE), bf16)] * 3
        + [pltpu.VMEM((heads, length, WIDE), bf16) for length in lengths] * 2
        + [pltpu.VMEM((heads, WIDE, length), bf16) for length in lengths]
        + [pltpu.VMEM((heads, length, WIDE), bf16) for length in lengths] * 2,
        compiler_params=pltpu.CompilerParams(vmem_limit_bytes=56 * 1024 * 1024),
        cost_estimate=pl.CostEstimate(
            flops=10 * heads * rows * total * 256,
            bytes_accessed=8 * (rows + total) * width,
            transcendentals=heads * rows * total,
        ),
    )(info, query, d_out, lse, *keys, *values, *earlier)
    return results[0], results[1 : 1 + parts], results[1 + parts :]


def contract_kernel(left, right, out, turned):
    @pl.when(pl.program_id(0) == 0)
    def _():
        turned[...] = jnp.transpose(left[...])

    out[...] = nn(turned[...], right[...]).astype(bf16)


def contract_rows(left, right, block=512):
    rows, width = left.shape
    columns = right.shape[1]
    block = min(block, columns)
    return pl.pallas_call(
        contract_kernel,
        grid=(pl.cdiv(columns, block),),
        in_specs=[
            pl.BlockSpec((rows, width), lambda step: (0, 0)),
            pl.BlockSpec((rows, block), lambda step: (0, step)),
        ],
        out_specs=pl.BlockSpec((width, block), lambda step: (0, step)),
        out_shape=jax.ShapeDtypeStruct((width, columns), bf16),
        scratch_shapes=[pltpu.VMEM((width, rows), bf16)],
        compiler_params=pltpu.CompilerParams(vmem_limit_bytes=40 * 1024 * 1024),
        cost_estimate=pl.CostEstimate(
            flops=2 * rows * width * columns,
            bytes_accessed=2 * (rows * width + (rows + width) * columns),
            transcendentals=0,
        ),
    )(left, right)


def column_sum(tensor):
    return jnp.sum(tensor.astype(f32), axis=0)


def after(value, *earlier):
    return lax.optimization_barrier((value, *earlier))[0]


def together(*values):
    return lax.optimization_barrier(values)


def norm_parts(tensor):
    centered = tensor - jnp.mean(tensor, axis=-1, keepdims=True)
    scale = lax.rsqrt(jnp.mean(centered * centered, axis=-1, keepdims=True) + epsilon)
    return centered * scale, scale


def norm_back(upstream, normal, scale, gain):
    weighted = upstream * gain
    mean_one = jnp.mean(weighted, axis=-1, keepdims=True)
    mean_two = jnp.mean(weighted * normal, axis=-1, keepdims=True)
    return scale * (weighted - mean_one - normal * mean_two)


def gelu_and_slope(tensor):
    square = tensor * tensor
    bent = jnp.tanh(0.7978845608028654 * tensor * (1.0 + 0.044715 * square))
    half = 0.5 * (1.0 + bent)
    slope = half + 0.5 * tensor * (1.0 - bent * bent) * 0.7978845608028654 * (
        1.0 + 0.134145 * square
    )
    return tensor * half, slope


def place_kernel(count, slots, *refs):
    pieces, (out, sems) = refs[:count], refs[-2:]
    copies = []
    for piece in pieces:
        for line in range(piece.shape[0]):
            for part in range(piece.shape[1]):
                index = len(copies)
                copies.append(
                    pltpu.make_async_copy(
                        piece.at[line, part], out.at[slots[index]], sems.at[index]
                    )
                )
    for copy in copies:
        copy.start()
    for copy in copies:
        copy.wait()


def place(pieces, slots, earlier=()):
    rows, columns = pieces[0].shape[2:]
    total = sum(piece.shape[0] * piece.shape[1] for piece in pieces)
    return pl.pallas_call(
        functools.partial(place_kernel, len(pieces)),
        in_specs=[pl.BlockSpec(memory_space=pltpu.SMEM)]
        + anywhere(pieces)
        + anywhere(earlier),
        out_specs=pl.BlockSpec(memory_space=pltpu.VMEM),
        out_shape=jax.ShapeDtypeStruct((total, rows, columns), pieces[0].dtype),
        scratch_shapes=[pltpu.SemaphoreType.DMA((total,))],
        compiler_params=pltpu.CompilerParams(vmem_limit_bytes=32 * 1024 * 1024),
        cost_estimate=pl.CostEstimate(
            flops=0, bytes_accessed=4 * total * rows * columns, transcendentals=0
        ),
    )(slots, *pieces, *earlier)


class Grid:
    def __init__(self, shard_rows):
        self.size = lax.axis_size("fsdp")
        self.apart = HD // shard_rows
        self.depth = self.size // 4
        me = lax.axis_index("fsdp")
        self.twin = (me // self.apart) % 2
        member = (me // (2 * self.apart)) * self.apart + me % self.apart
        self.z, self.x = member // 2, member % 2

    def index(self, z, x, twin):
        member = z * 2 + x
        return (
            (member // self.apart) * 2 * self.apart + twin * self.apart + member % self.apart
        )

    def pairs(self, step_z=0, step_x=0, step_twin=0):
        return [
            (
                self.index(z, x, twin),
                self.index((z + step_z) % self.depth, x ^ step_x, twin ^ step_twin),
            )
            for z in range(self.depth)
            for x in range(2)
            for twin in range(2)
        ]

    def send(self, value, **steps):
        return lax.ppermute(value, "fsdp", self.pairs(**steps))

    def members(self):
        return [
            ((self.z + step_z) % self.depth) * 2 + (self.x ^ step_x)
            for step_x in range(2)
            for step_z in range(self.depth)
        ]

    def shards(self):
        return [
            (member // self.apart) * 2 * self.apart
            + (self.twin ^ step) * self.apart
            + member % self.apart
            for member in self.members()
            for step in range(2)
        ]

    def kinds_by_seq(self):
        kinds = [
            [self.index(member // 2, member % 2, twin) for member in range(2 * self.depth)]
            for twin in range(2)
        ]
        first = lax.axis_index("seq") == 0
        return [jnp.where(first, one, two) for one, two in zip(*kinds)] + [
            jnp.where(first, two, one) for one, two in zip(*kinds)
        ]

    def shards_by_seq(self):
        mine = self.shards()
        first = lax.axis_index("seq") == 0
        kinds = [mine[0::2], mine[1::2]]
        return [jnp.where(first, one, two) for one, two in zip(*kinds)] + [
            jnp.where(first, two, one) for one, two in zip(*kinds)
        ]

    def groups(self):
        return [
            [self.index(member // 2, member % 2, twin) for member in range(2 * self.depth)]
            for twin in range(2)
        ]

    def gather(self, block):
        whole = lax.all_gather(block, "fsdp", axis_index_groups=self.groups())
        _, _, rows, columns = whole.shape
        whole = whole.reshape(-1, self.apart, 2, rows, columns).transpose(0, 2, 1, 3, 4)
        return whole.reshape(-1, columns)

    def scatter(self, matrix):
        columns = matrix.shape[1]
        matrix = matrix.reshape(2 * self.depth // self.apart, 2, self.apart, -1, columns)
        matrix = matrix.transpose(0, 2, 1, 3, 4).reshape(-1, columns)
        return lax.psum_scatter(
            matrix, "fsdp", scatter_dimension=0, axis_index_groups=self.groups(), tiled=True
        )

    def own_half(self, halves):
        return jnp.where(self.twin == 0, halves[0], halves[1])

    def other_half(self, halves):
        return jnp.where(self.twin == 0, halves[1], halves[0])

    def swap_rows(self, partial, rows):
        sent = jnp.concatenate([partial[rows:], partial[:rows]], axis=0).astype(bf16)
        return self.send(sent, step_twin=1).astype(f32)

    def swap_mine(self, first, second):
        mine, sent = self.in_order(first, second)
        return self.in_order(mine, self.send(sent.astype(bf16), step_twin=1).astype(f32))

    def in_order(self, mine, other):
        first = self.twin == 0
        return jnp.where(first, mine, other), jnp.where(first, other, mine)


def order_matrix(places, rows):
    count = len(places) * rows
    source = (jnp.stack(places) * rows)[:, None] + jnp.arange(rows, dtype=jnp.int32)[None, :]
    return (jnp.arange(count, dtype=jnp.int32)[:, None] == source.reshape(1, count)).astype(bf16)


def reorder(rows, matrix):
    half = matrix.shape[1] // 2
    return [
        jnp.dot(rows, part, preferred_element_type=f32).astype(bf16)
        for part in (matrix[:, :half], matrix[:, half:])
    ]


def gather_z(grid, block):
    sent = {step: grid.send(block, step_z=step) for step in range(1, grid.depth)}
    return [block] + [sent[grid.depth - step] for step in range(1, grid.depth)]


def gather_x(grid, blocks):
    joined = jnp.stack(blocks)
    return joined, grid.send(joined, step_x=1)


def gather_all(grid, block):
    lines = gather_z(grid, block)
    return lines, list(gather_x(grid, lines))


def by_seq(first_value, second_value):
    return jnp.where(lax.axis_index("seq") == 0, first_value, second_value)


def gather_by_seq(grid, block, *beside):
    lines = gather_z(grid, by_seq(block[:1], block[1:]))
    joined, *beside = together(jnp.stack(lines), *beside)
    across = grid.send(joined, step_x=1)
    return lines, [joined, across, swap_seq(joined), swap_seq(across)], beside


def halves_of(left, right):
    going = contract_rows(left[1], right)
    return contract_rows(left[0], right), going


def add_pieces(kept, came, count):
    rows = kept.shape[0] // count
    return [
        (
            kept[step * rows : (step + 1) * rows].astype(f32)
            + came[step * rows : (step + 1) * rows].astype(f32)
        ).astype(bf16)
        for step in range(count)
    ]


def swap_seq(value):
    return lax.ppermute(value, "seq", [(0, 1), (1, 0)])


def sum_z(grid, sums):
    total = sums[0].astype(f32)
    for step in range(1, grid.depth):
        total = total + grid.send(sums[step], step_z=step).astype(f32)
    return total.astype(bf16)


class ScatterX:
    def __init__(self, grid, left, right):
        self.grid = grid
        self.kept, self.going = halves_of(left, right)
        self.came = grid.send(self.going, step_x=1)

    def add(self):
        self.sums = add_pieces(self.kept, self.came, self.grid.depth)
        return self.sums

    def finish(self):
        return sum_seq(sum_z(self.grid, self.sums))


class ScatterY:
    def __init__(self, grid, left, right):
        self.grid = grid
        self.kept, self.going = halves_of(left, right)
        self.came = swap_seq(self.going)

    def cross(self):
        self.kept, self.going = add_pieces(self.kept, self.came, 2)
        self.came = self.grid.send(self.going, step_x=1)
        return [self.kept, self.going]

    def add(self):
        self.sums = add_pieces(self.kept, self.came, self.grid.depth)
        return self.sums

    def finish(self):
        total = sum_z(self.grid, self.sums)
        other = swap_seq(total)
        first = lax.axis_index("seq") == 0
        return jnp.concatenate(
            [jnp.where(first, total, other), jnp.where(first, other, total)], axis=0
        ).astype(f32)


def sum_seq(value):
    groups = lax.axis_size("seq")
    if groups == 2:
        return value.astype(f32) + lax.ppermute(value, "seq", [(0, 1), (1, 0)]).astype(f32)
    return lax.psum(value.astype(f32), "seq")


def swap_twin(grid, total):
    rows = total.shape[0] // 2
    other = grid.send(total[rows:].astype(bf16), step_twin=1).astype(f32)
    return grid.in_order(total[:rows], other)


def sum_all(vector):
    for axis in ("fsdp", "seq"):
        count = lax.axis_size(axis)
        step = 1
        while step < count:
            vector = vector + lax.ppermute(
                vector, axis, [(member, member ^ step) for member in range(count)]
            )
            step *= 2
    return vector


def body(
    tokens,
    lengths,
    cotangent,
    attn_gain,
    attn_shift,
    qkv_weight,
    query_bias,
    value_bias,
    out_weight,
    out_bias,
    mlp_gain,
    mlp_shift,
    up_weight,
    up_bias,
    down_weight,
    down_bias,
):
    groups = lax.axis_size("seq")
    images, local_len, width = tokens.shape
    shard_rows = qkv_weight.shape[0]
    hidden_half = up_weight.shape[1] // 2
    rows = images * local_len
    heads = width // HD
    own_width = width // 2
    grid = Grid(shard_rows)
    all_members = jnp.stack(grid.members())

    def by_kind(matrix):
        lead = matrix.shape[0]
        split = matrix.reshape(lead, -1, heads // 2, 2, HD)
        return [split[:, :, :, kind].reshape(lead, -1) for kind in range(2)]

    def vector_kind(vector):
        return grid.own_half([vector.reshape(-1, 2, HD)[:, kind].reshape(-1) for kind in range(2)])

    def two_halves(matrix):
        return [matrix[:, :hidden_half], matrix[:, hidden_half:]]

    def pair_up(halves):
        other = grid.send(grid.other_half(halves), step_twin=1)
        return jnp.stack([grid.own_half(halves), other])

    def both(value):
        flat = value.reshape(rows, width)
        return jnp.concatenate([flat, grid.send(flat, step_twin=1)], axis=0)

    qkv_block = pair_up(by_kind(qkv_weight))
    pair_block = qkv_block[:, :, own_width:]
    all_kinds = jnp.stack(grid.shards())
    order = order_matrix(grid.shards(), shard_rows)
    own_order = order_matrix(grid.members(), shard_rows)
    inputs = both(tokens).astype(f32)
    normal_one, scale_one = norm_parts(inputs)
    normed_one = (normal_one * attn_gain + attn_shift).astype(bf16)
    up_weight, down_turned = after((up_weight, down_weight.T), qkv_block)
    up_block = jnp.stack(grid.in_order(*pair_up(two_halves(up_weight))))
    down_block = jnp.stack(grid.in_order(*pair_up(two_halves(down_turned))))
    sizes = jnp.concatenate([lengths, grid.send(lengths, step_twin=1)])
    if groups == 2:
        scatter_seq, seq_order = ScatterY, order_matrix(grid.shards_by_seq(), shard_rows)
        pair_lines, pair_pieces, (normed_one, up_block, down_block, sizes) = gather_by_seq(
            grid, pair_block, normed_one, up_block, down_block, sizes
        )
        pair_slots = jnp.stack(grid.shards_by_seq())
    else:
        scatter_seq, seq_order = ScatterX, order
        pair_lines, pair_pieces = gather_all(grid, pair_block)
        pair_slots = all_kinds
    query_lines, query_pieces = gather_all(
        grid, after(qkv_block[:, :, :own_width], *pair_lines[1:])
    )
    out_lines, out_pieces = gather_all(grid, after(out_weight[None], *query_lines[1:]))

    down_block = after(down_block, pair_pieces[1])
    if groups == 2:
        kinds_by_seq = jnp.stack(grid.kinds_by_seq())
        own_down = lax.all_gather(
            by_seq(down_block[0], down_block[1])[None],
            "fsdp",
            axis_index_groups=grid.groups(),
        )
        own_down = [own_down, swap_seq(own_down)]
    else:
        own_down = grid.gather(down_block)
    up_block = after(up_block, *query_lines[1:])
    own_up = grid.gather(up_block)

    back_low = both(cotangent)

    own_pair = place(pair_pieces, pair_slots, query_lines[1:]).reshape(width, 2 * own_width)
    pair_bias = jnp.concatenate([jnp.zeros((own_width,), f32), vector_kind(value_bias)])
    pairs = (jnp.dot(normed_one, own_pair, preferred_element_type=f32) + pair_bias).astype(bf16)
    own_query = place(query_pieces, all_kinds, out_lines[1:])
    own_query = own_query.reshape(width, own_width)
    queries = (
        jnp.dot(normed_one, own_query, preferred_element_type=f32) + vector_kind(query_bias)
    ).astype(bf16)

    one_rows = reorder(normed_one, order)
    seq_rows = reorder(normed_one, seq_order) if groups == 2 else one_rows
    kind_rows = []
    if groups == 2:
        kind_rows = reorder(back_low, order_matrix(grid.kinds_by_seq(), shard_rows))
    made = [*one_rows, *seq_rows, *kind_rows]

    place_seq = lax.axis_index("seq") * local_len
    attended_parts, saved = [], []
    for image in range(2 * images):
        span = slice(image * local_len, (image + 1) * local_len)
        query, near = queries[span][None], pairs[span][None]
        key, value = near[:, :, :own_width], near[:, :, own_width:]
        if groups == 2:
            far = swap_seq(near)
            key_parts = (key, far[:, :, :own_width])
            value_parts = (value, far[:, :, own_width:])
            info = jnp.stack([sizes[image], place_seq, local_len - place_seq])
        else:
            key_parts = (lax.all_gather(key, "seq", axis=1, tiled=True),)
            value_parts = (lax.all_gather(value, "seq", axis=1, tiled=True),)
            info = jnp.stack([sizes[image], jnp.zeros_like(sizes[image])])
        attended_part, lse = attend(
            info, query, key_parts, value_parts, made if image == 0 else ()
        )
        attended_parts.append(attended_part[0])
        saved.append((info, query, key_parts, value_parts, lse))
    attended = jnp.concatenate(attended_parts, axis=0)

    own_out = place(out_pieces, all_members)
    own_out = own_out.reshape(own_width, width)
    partial = jnp.dot(attended, own_out, preferred_element_type=f32)
    resid = inputs + partial + grid.swap_rows(partial, rows) + out_bias
    normal_two, scale_two = norm_parts(resid)
    normed_two = (normal_two * mlp_gain + mlp_shift).astype(bf16)
    own_up_bias = grid.own_half([up_bias[:hidden_half], up_bias[hidden_half:]])
    if groups == 2:
        normed_two, own_down[1] = together(normed_two, own_down[1])
    hidden = jnp.dot(normed_two, own_up, preferred_element_type=f32) + own_up_bias
    active, slope = gelu_and_slope(hidden)
    active, slope = lax.optimization_barrier((active.astype(bf16), slope.astype(bf16)))
    if groups == 2:
        down_kept, down_going = halves_of(kind_rows, active)
        down_came = swap_seq(down_going)
        own_down = place(own_down, kinds_by_seq, [down_kept, down_going])
        own_down = own_down.reshape(width, hidden_half)
    else:
        grad_down = grid.scatter(contract_rows(back_low, active))

    d_active = jnp.dot(back_low, own_down, preferred_element_type=f32)
    d_hidden = (d_active * slope).astype(bf16)
    grad_up = contract_rows(normed_two, d_hidden)
    d_hidden, grad_up = lax.optimization_barrier((d_hidden, grad_up))
    grad_up = grid.scatter(grad_up)
    partial = lax.dot_general(
        d_hidden, own_up, (((1,), (1,)), ((), ())), preferred_element_type=f32
    )
    d_two = partial + grid.swap_rows(partial, rows)
    d_resid = back_low.astype(f32) + norm_back(d_two, normal_two, scale_two, mlp_gain)
    out_low = d_resid.astype(bf16)
    grad_out = ScatterX(grid, reorder(attended, own_order), out_low)
    d_attended = lax.dot_general(
        out_low, own_out, (((1,), (1,)), ((), ())), preferred_element_type=f32
    ).astype(bf16)

    d_query, d_key, d_value = [], [], []
    for image in range(2 * images):
        span = slice(image * local_len, (image + 1) * local_len)
        info, query, key_parts, value_parts, lse = saved[image]
        if image == 0:
            on_their_way = [grad_out.kept, grad_out.going]
        elif image == images and groups == 2:
            on_their_way = add_pieces(down_kept, down_came, 1)
            down_total = on_their_way[0]
        else:
            on_their_way = []
        d_query_part, key_grads, value_grads = attend_back(
            info,
            query,
            d_attended[span][None],
            lse,
            key_parts,
            value_parts,
            on_their_way,
        )
        d_query.append(d_query_part[0])
        if groups == 2:
            near = jnp.concatenate([key_grads[1], value_grads[1]], axis=2)
            d_query[-1], near = together(d_query[-1], near)
            far = swap_seq(near)
            if image == 2 * images - 1:
                last_far = far
            d_key.append((key_grads[0], far[:, :, :own_width]))
            d_value.append((value_grads[0], far[:, :, own_width:]))
        else:
            for into, member in ((d_key, key_grads[0]), (d_value, value_grads[0])):
                into.append(
                    (
                        lax.psum_scatter(
                            member.astype(f32), "seq", scatter_dimension=1, tiled=True
                        ),
                    )
                )
    d_query = jnp.concatenate(d_query, axis=0)
    grad_query = ScatterX(grid, one_rows, d_query)
    late_active, grad_query.kept, grad_query.going = together(
        active, grad_query.kept, grad_query.going
    )
    partial = lax.dot_general(
        late_active, own_down, (((1,), (1,)), ((), ())), preferred_element_type=f32
    )
    came = grid.send(partial[rows:].astype(bf16), step_twin=1).astype(f32)
    outputs = (resid[:rows] + partial[:rows] + came + down_bias).astype(bf16)
    grad_out.add()
    grad_query.add()
    if groups == 2:
        last_far, grad_up, *grad_query.sums = together(last_far, grad_up, *grad_query.sums)
        d_key[-1] = (d_key[-1][0], last_far[:, :, :own_width])
        d_value[-1] = (d_value[-1][0], last_far[:, :, own_width:])

    d_key, d_value = (
        jnp.concatenate(
            [sum(part.astype(f32) for part in parts)[0].astype(bf16) for parts in member], axis=0
        )
        for member in (d_key, d_value)
    )
    grad_key = scatter_seq(grid, seq_rows, d_key)
    grad_value = ScatterX(grid, one_rows, d_value)
    d_query, d_key, d_value, grad_key.kept, grad_key.going, grad_value.kept, grad_value.going = (
        together(
            d_query,
            d_key,
            d_value,
            grad_key.kept,
            grad_key.going,
            grad_value.kept,
            grad_value.going,
        )
    )
    partial = sum(
        lax.dot_general(member, weight, (((1,), (1,)), ((), ())), preferred_element_type=f32)
        for member, weight in (
            (d_query, own_query),
            (d_key, own_pair[:, :own_width]),
            (d_value, own_pair[:, own_width:]),
        )
    )
    d_one = partial[:rows] + grid.send(partial[rows:].astype(bf16), step_twin=1).astype(f32)
    grad_value.add()
    if groups == 2:
        grad_key.cross()
        d_one, grad_key.going, *grad_value.sums = together(
            d_one, grad_key.going, *grad_value.sums
        )
    grad_tokens = d_resid[:rows] + norm_back(d_one, normal_one[:rows], scale_one[:rows], attn_gain)
    grad_key.add()
    grad_out = grad_out.finish()
    grad_up = sum_seq(grad_up)
    if groups == 2:
        grad_down = lax.psum_scatter(
            down_total,
            "fsdp",
            scatter_dimension=0,
            axis_index_groups=grid.groups(),
            tiled=True,
        )
        grad_down, *grad_key.sums = together(grad_down, *grad_key.sums)
        other = swap_seq(grad_down)
        grad_down = by_seq(
            jnp.concatenate([grad_down, other]), jnp.concatenate([other, grad_down])
        ).astype(f32)
    else:
        grad_down = sum_seq(grad_down)
    grad_qkv = jnp.concatenate(
        [grad_query.finish(), grad_key.finish(), grad_value.finish()], axis=1
    )

    grad_up, grad_down = (
        jnp.concatenate(grid.swap_mine(total[:shard_rows], total[shard_rows:]), axis=1)
        for total in (grad_up, grad_down)
    )
    grad_down = grad_down.T
    grad_qkv = jnp.stack(
        [member.reshape(shard_rows, 3, heads // 2, HD) for member in swap_twin(grid, grad_qkv)],
        axis=3,
    ).reshape(shard_rows, 3 * width)

    def at_kind(vector, shape, axis):
        vector = vector.reshape(shape)
        nothing = jnp.zeros_like(vector)
        return jnp.stack(grid.in_order(vector, nothing), axis=axis).reshape(-1)

    vectors = sum_all(
        jnp.concatenate(
            [
                column_sum(d_one * normal_one[:rows]),
                column_sum(d_one),
                at_kind(column_sum(d_query), (heads // 2, HD), 1),
                at_kind(column_sum(d_value), (heads // 2, HD), 1),
                column_sum(out_low[:rows]),
                column_sum(d_two[:rows] * normal_two[:rows]),
                column_sum(d_two[:rows]),
                column_sum(back_low[:rows]),
                at_kind(column_sum(d_hidden), (-1,), 0),
            ]
        )
    )
    (
        grad_attn_gain,
        grad_attn_shift,
        grad_query_bias,
        grad_value_bias,
        grad_out_bias,
        grad_mlp_gain,
        grad_mlp_shift,
        grad_down_bias,
    ) = (vectors[step * width : (step + 1) * width] for step in range(8))
    grad_up_bias = vectors[8 * width :]
    shape = (images, local_len, width)
    return (
        outputs.reshape(shape),
        grad_tokens.reshape(shape),
        grad_attn_gain,
        grad_attn_shift,
        grad_qkv,
        grad_query_bias,
        grad_value_bias,
        grad_out,
        grad_out_bias,
        grad_mlp_gain,
        grad_mlp_shift,
        grad_up,
        grad_up_bias,
        grad_down,
        grad_down_bias,
    )


def solution(mesh):
    return jax.shard_map(
        body,
        mesh=mesh,
        in_specs=(
            P("fsdp", "seq", None),
            P("fsdp"),
            P("fsdp", "seq", None),
            P(),
            P(),
            P("fsdp", None),
            P(),
            P(),
            P("fsdp", None),
            P(),
            P(),
            P(),
            P("fsdp", None),
            P(),
            P(None, "fsdp"),
            P(),
        ),
        out_specs=(
            P("fsdp", "seq", None),
            P("fsdp", "seq", None),
            P(),
            P(),
            P("fsdp", None),
            P(),
            P(),
            P("fsdp", None),
            P(),
            P(),
            P(),
            P("fsdp", None),
            P(),
            P(None, "fsdp"),
            P(),
        ),
        check_vma=False,
    )
```

```python
import functools

import jax
import jax.numpy as jnp
from jax import lax
from jax.experimental import pallas as pl
from jax.experimental.pallas import tpu as pltpu
from jax.sharding import PartitionSpec as P

HD = 72
WIDE = 128
SCALE = HD ** (-0.5)
masked_score = -1e30
epsilon = 1e-06
f32, bf16 = jnp.float32, jnp.bfloat16


def spread_heads(source, target, heads):
    for head in range(heads):
        target[head, :, :HD] = source[0, :, head * HD : (head + 1) * HD]


def turn_heads(source, target, heads):
    for head in range(heads):
        target[head] = jnp.transpose(source[head])


def join_heads(source, heads):
    return jnp.concatenate([source[head, :, :HD] for head in range(heads)], axis=1)


def nt(left, right):
    return lax.dot_general(left, right, (((1,), (1,)), ((), ())), preferred_element_type=f32)


def nn(left, right):
    return jnp.dot(left, right, preferred_element_type=f32)


def attend_kernel(parts, heads, block, earlier, info, *refs):
    q_in = refs[0]
    k_in = refs[1 : 1 + parts]
    v_in = refs[1 + parts : 1 + 2 * parts]
    refs = refs[1 + 2 * parts + earlier :]
    out, lse = refs[:2]
    scratch = refs[2:]
    q_s, o_s = scratch[:2]
    k_s = scratch[2 : 2 + parts]
    vt_s = scratch[2 + parts : 2 + 2 * parts]
    head = pl.program_id(0)
    rows = q_s.shape[1]

    @pl.when(head == 0)
    def _():
        q_s[...] = jnp.zeros_like(q_s)
        spread_heads(q_in, q_s, heads)
        for part in range(parts):
            k_s[part][...] = jnp.zeros_like(k_s[part])
            spread_heads(v_in[part], k_s[part], heads)
            turn_heads(k_s[part], vt_s[part], heads)
            spread_heads(k_in[part], k_s[part], heads)

    masks = []
    for part in range(parts):
        length = k_s[part].shape[1]
        masks.append(
            info[1 + part] + lax.broadcasted_iota(jnp.int32, (length, 1), 0) < info[0]
        )
    for start in range(0, rows, block):
        q_rows = q_s[head, start : start + block]
        scores = [
            jnp.where(masks[part], nt(k_s[part][head], q_rows), masked_score)
            for part in range(parts)
        ]
        peak = functools.reduce(
            jnp.maximum, [jnp.max(member, axis=0, keepdims=True) for member in scores]
        )
        total = 0.0
        result = 0.0
        for part in range(parts):
            grown = jnp.exp((scores[part] - peak) * SCALE)
            total = total + jnp.sum(grown, axis=0, keepdims=True)
            result = result + nn(vt_s[part][head], grown.astype(bf16))
        result = result / total
        o_s[head, start : start + block] = jnp.transpose(result).astype(bf16)
        lse[0, :, start : start + block] = peak * SCALE + jnp.log(total)

    @pl.when(head == heads - 1)
    def _():
        out[0] = join_heads(o_s, heads)


def attend_back_kernel(parts, heads, block, earlier, info, *refs):
    q_in, d_in, lse = refs[:3]
    k_in = refs[3 : 3 + parts]
    v_in = refs[3 + parts : 3 + 2 * parts]
    refs = refs[3 + 2 * parts + earlier :]
    dq_out = refs[0]
    dk_out = refs[1 : 1 + parts]
    dv_out = refs[1 + parts : 1 + 2 * parts]
    refs = refs[1 + 2 * parts :]
    q_s, d_s, dq_s = refs[:3]
    refs = refs[3:]
    k_s, v_s, kt_s, dk_s, dv_s = (refs[i * parts : (i + 1) * parts] for i in range(5))
    head = pl.program_id(0)
    rows = q_s.shape[1]

    @pl.when(head == 0)
    def _():
        q_s[...] = jnp.zeros_like(q_s)
        d_s[...] = jnp.zeros_like(d_s)
        spread_heads(q_in, q_s, heads)
        spread_heads(d_in, d_s, heads)
        for part in range(parts):
            k_s[part][...] = jnp.zeros_like(k_s[part])
            v_s[part][...] = jnp.zeros_like(v_s[part])
            spread_heads(k_in[part], k_s[part], heads)
            spread_heads(v_in[part], v_s[part], heads)
            turn_heads(k_s[part], kt_s[part], heads)

    masks = []
    for part in range(parts):
        length = k_s[part].shape[1]
        masks.append(
            info[1 + part] + lax.broadcasted_iota(jnp.int32, (length, 1), 0) < info[0]
        )
    d_key = [0.0] * parts
    d_value = [0.0] * parts
    for start in range(0, rows, block):
        q_rows = q_s[head, start : start + block]
        d_rows = d_s[head, start : start + block]
        level = lse[0, :, start : start + block]
        probs = []
        d_probs = []
        row_dot = 0.0
        for part in range(parts):
            scores = jnp.where(masks[part], nt(k_s[part][head], q_rows) * SCALE, masked_score)
            probs.append(jnp.exp(scores - level))
            d_probs.append(nt(v_s[part][head], d_rows))
            row_dot = row_dot + jnp.sum(probs[part] * d_probs[part], axis=0, keepdims=True)
        d_query = 0.0
        for part in range(parts):
            d_scores = (probs[part] * (d_probs[part] - row_dot)).astype(bf16)
            d_value[part] = d_value[part] + nn(probs[part].astype(bf16), d_rows)
            d_key[part] = d_key[part] + nn(d_scores, q_rows)
            d_query = d_query + nn(kt_s[part][head], d_scores)
        dq_s[head, start : start + block] = jnp.transpose(d_query * SCALE).astype(bf16)
    for part in range(parts):
        dk_s[part][head] = (d_key[part] * SCALE).astype(bf16)
        dv_s[part][head] = d_value[part].astype(bf16)

    @pl.when(head == heads - 1)
    def _():
        dq_out[0] = join_heads(dq_s, heads)
        for part in range(parts):
            dk_out[part][0] = join_heads(dk_s[part], heads)
            dv_out[part][0] = join_heads(dv_s[part], heads)


def whole(shape):
    return pl.BlockSpec(shape, lambda head: (0,) * len(shape))


def anywhere(arrays):
    return [pl.BlockSpec(memory_space=pl.ANY)] * len(arrays)


def attend(info, query, keys, values, earlier=(), block=512):
    _, rows, width = query.shape
    heads = width // HD
    parts = len(keys)
    lengths = [member.shape[1] for member in keys]
    total = sum(lengths)
    return pl.pallas_call(
        functools.partial(attend_kernel, parts, heads, min(block, rows), len(earlier)),
        grid=(heads,),
        in_specs=[pl.BlockSpec(memory_space=pltpu.SMEM), whole(query.shape)]
        + [whole(member.shape) for member in (*keys, *values)]
        + anywhere(earlier),
        out_specs=[whole(query.shape), pl.BlockSpec((1, 1, rows), lambda head: (head, 0, 0))],
        out_shape=[
            jax.ShapeDtypeStruct(query.shape, bf16),
            jax.ShapeDtypeStruct((heads, 1, rows), f32),
        ],
        scratch_shapes=[pltpu.VMEM((heads, rows, WIDE), bf16)] * 2
        + [pltpu.VMEM((heads, length, WIDE), bf16) for length in lengths]
        + [pltpu.VMEM((heads, WIDE, length), bf16) for length in lengths],
        compiler_params=pltpu.CompilerParams(vmem_limit_bytes=48 * 1024 * 1024),
        cost_estimate=pl.CostEstimate(
            flops=4 * heads * rows * total * 256,
            bytes_accessed=4 * (rows + total) * width,
            transcendentals=heads * rows * total,
        ),
    )(info, query, *keys, *values, *earlier)


def attend_back(info, query, d_out, lse, keys, values, earlier=(), block=256):
    _, rows, width = query.shape
    heads = width // HD
    parts = len(keys)
    lengths = [member.shape[1] for member in keys]
    total = sum(lengths)
    results = pl.pallas_call(
        functools.partial(attend_back_kernel, parts, heads, min(block, rows), len(earlier)),
        grid=(heads,),
        in_specs=[
            pl.BlockSpec(memory_space=pltpu.SMEM),
            whole(query.shape),
            whole(query.shape),
            pl.BlockSpec((1, 1, rows), lambda head: (head, 0, 0)),
        ]
        + [whole(member.shape) for member in (*keys, *values)]
        + anywhere(earlier),
        out_specs=[whole(member.shape) for member in (query, *keys, *values)],
        out_shape=[
            jax.ShapeDtypeStruct(member.shape, bf16) for member in (query, *keys, *values)
        ],
        scratch_shapes=[pltpu.VMEM((heads, rows, WIDE), bf16)] * 3
        + [pltpu.VMEM((heads, length, WIDE), bf16) for length in lengths] * 2
        + [pltpu.VMEM((heads, WIDE, length), bf16) for length in lengths]
        + [pltpu.VMEM((heads, length, WIDE), bf16) for length in lengths] * 2,
        compiler_params=pltpu.CompilerParams(vmem_limit_bytes=56 * 1024 * 1024),
        cost_estimate=pl.CostEstimate(
            flops=10 * heads * rows * total * 256,
            bytes_accessed=8 * (rows + total) * width,
            transcendentals=heads * rows * total,
        ),
    )(info, query, d_out, lse, *keys, *values, *earlier)
    return results[0], results[1 : 1 + parts], results[1 + parts :]


def contract_kernel(left, right, out, turned):
    @pl.when(pl.program_id(0) == 0)
    def _():
        turned[...] = jnp.transpose(left[...])

    out[...] = nn(turned[...], right[...]).astype(bf16)


def contract_rows(left, right, block=512):
    rows, width = left.shape
    columns = right.shape[1]
    block = min(block, columns)
    return pl.pallas_call(
        contract_kernel,
        grid=(pl.cdiv(columns, block),),
        in_specs=[
            pl.BlockSpec((rows, width), lambda step: (0, 0)),
            pl.BlockSpec((rows, block), lambda step: (0, step)),
        ],
        out_specs=pl.BlockSpec((width, block), lambda step: (0, step)),
        out_shape=jax.ShapeDtypeStruct((width, columns), bf16),
        scratch_shapes=[pltpu.VMEM((width, rows), bf16)],
        compiler_params=pltpu.CompilerParams(vmem_limit_bytes=40 * 1024 * 1024),
        cost_estimate=pl.CostEstimate(
            flops=2 * rows * width * columns,
            bytes_accessed=2 * (rows * width + (rows + width) * columns),
            transcendentals=0,
        ),
    )(left, right)


def column_sum(tensor):
    return jnp.sum(tensor.astype(f32), axis=0)


def after(value, *earlier):
    return lax.optimization_barrier((value, *earlier))[0]


def together(*values):
    return lax.optimization_barrier(values)


def norm_parts(tensor):
    centered = tensor - jnp.mean(tensor, axis=-1, keepdims=True)
    scale = lax.rsqrt(jnp.mean(centered * centered, axis=-1, keepdims=True) + epsilon)
    return centered * scale, scale


def norm_back(upstream, normal, scale, gain):
    weighted = upstream * gain
    mean_one = jnp.mean(weighted, axis=-1, keepdims=True)
    mean_two = jnp.mean(weighted * normal, axis=-1, keepdims=True)
    return scale * (weighted - mean_one - normal * mean_two)


def gelu_and_slope(tensor):
    square = tensor * tensor
    bent = jnp.tanh(0.7978845608028654 * tensor * (1.0 + 0.044715 * square))
    half = 0.5 * (1.0 + bent)
    slope = half + 0.5 * tensor * (1.0 - bent * bent) * 0.7978845608028654 * (
        1.0 + 0.134145 * square
    )
    return tensor * half, slope


def place_kernel(count, slots, *refs):
    pieces, (out, sems) = refs[:count], refs[-2:]
    copies = []
    for piece in pieces:
        for line in range(piece.shape[0]):
            for part in range(piece.shape[1]):
                index = len(copies)
                copies.append(
                    pltpu.make_async_copy(
                        piece.at[line, part], out.at[slots[index]], sems.at[index]
                    )
                )
    for copy in copies:
        copy.start()
    for copy in copies:
        copy.wait()


def place(pieces, slots, earlier=()):
    rows, columns = pieces[0].shape[2:]
    total = sum(piece.shape[0] * piece.shape[1] for piece in pieces)
    return pl.pallas_call(
        functools.partial(place_kernel, len(pieces)),
        in_specs=[pl.BlockSpec(memory_space=pltpu.SMEM)]
        + anywhere(pieces)
        + anywhere(earlier),
        out_specs=pl.BlockSpec(memory_space=pltpu.VMEM),
        out_shape=jax.ShapeDtypeStruct((total, rows, columns), pieces[0].dtype),
        scratch_shapes=[pltpu.SemaphoreType.DMA((total,))],
        compiler_params=pltpu.CompilerParams(vmem_limit_bytes=32 * 1024 * 1024),
        cost_estimate=pl.CostEstimate(
            flops=0, bytes_accessed=4 * total * rows * columns, transcendentals=0
        ),
    )(slots, *pieces, *earlier)


class Grid:
    def __init__(self, shard_rows):
        self.size = lax.axis_size("fsdp")
        self.apart = HD // shard_rows
        self.depth = self.size // 4
        me = lax.axis_index("fsdp")
        self.twin = (me // self.apart) % 2
        member = (me // (2 * self.apart)) * self.apart + me % self.apart
        self.z, self.x = member // 2, member % 2

    def index(self, z, x, twin):
        member = z * 2 + x
        return (
            (member // self.apart) * 2 * self.apart + twin * self.apart + member % self.apart
        )

    def pairs(self, step_z=0, step_x=0, step_twin=0):
        return [
            (
                self.index(z, x, twin),
                self.index((z + step_z) % self.depth, x ^ step_x, twin ^ step_twin),
            )
            for z in range(self.depth)
            for x in range(2)
            for twin in range(2)
        ]

    def send(self, value, **steps):
        return lax.ppermute(value, "fsdp", self.pairs(**steps))

    def members(self):
        return [
            ((self.z + step_z) % self.depth) * 2 + (self.x ^ step_x)
            for step_x in range(2)
            for step_z in range(self.depth)
        ]

    def shards(self):
        return [
            (member // self.apart) * 2 * self.apart
            + (self.twin ^ step) * self.apart
            + member % self.apart
            for member in self.members()
            for step in range(2)
        ]

    def kinds_by_seq(self):
        kinds = [
            [self.index(member // 2, member % 2, twin) for member in range(2 * self.depth)]
            for twin in range(2)
        ]
        first = lax.axis_index("seq") == 0
        return [jnp.where(first, one, two) for one, two in zip(*kinds)] + [
            jnp.where(first, two, one) for one, two in zip(*kinds)
        ]

    def shards_by_seq(self):
        mine = self.shards()
        first = lax.axis_index("seq") == 0
        kinds = [mine[0::2], mine[1::2]]
        return [jnp.where(first, one, two) for one, two in zip(*kinds)] + [
            jnp.where(first, two, one) for one, two in zip(*kinds)
        ]

    def groups(self):
        return [
            [self.index(member // 2, member % 2, twin) for member in range(2 * self.depth)]
            for twin in range(2)
        ]

    def gather(self, block):
        whole = lax.all_gather(block, "fsdp", axis_index_groups=self.groups())
        _, _, rows, columns = whole.shape
        whole = whole.reshape(-1, self.apart, 2, rows, columns).transpose(0, 2, 1, 3, 4)
        return whole.reshape(-1, columns)

    def scatter(self, matrix):
        columns = matrix.shape[1]
        matrix = matrix.reshape(2 * self.depth // self.apart, 2, self.apart, -1, columns)
        matrix = matrix.transpose(0, 2, 1, 3, 4).reshape(-1, columns)
        return lax.psum_scatter(
            matrix, "fsdp", scatter_dimension=0, axis_index_groups=self.groups(), tiled=True
        )

    def own_half(self, halves):
        return jnp.where(self.twin == 0, halves[0], halves[1])

    def other_half(self, halves):
        return jnp.where(self.twin == 0, halves[1], halves[0])

    def swap_rows(self, partial, rows):
        sent = jnp.concatenate([partial[rows:], partial[:rows]], axis=0).astype(bf16)
        return self.send(sent, step_twin=1).astype(f32)

    def swap_mine(self, first, second):
        mine, sent = self.in_order(first, second)
        return self.in_order(mine, self.send(sent.astype(bf16), step_twin=1).astype(f32))

    def in_order(self, mine, other):
        first = self.twin == 0
        return jnp.where(first, mine, other), jnp.where(first, other, mine)


def order_matrix(places, rows):
    count = len(places) * rows
    source = (jnp.stack(places) * rows)[:, None] + jnp.arange(rows, dtype=jnp.int32)[None, :]
    return (jnp.arange(count, dtype=jnp.int32)[:, None] == source.reshape(1, count)).astype(bf16)


def reorder(rows, matrix):
    half = matrix.shape[1] // 2
    return [
        jnp.dot(rows, part, preferred_element_type=f32).astype(bf16)
        for part in (matrix[:, :half], matrix[:, half:])
    ]


def gather_z(grid, block):
    sent = {step: grid.send(block, step_z=step) for step in range(1, grid.depth)}
    return [block] + [sent[grid.depth - step] for step in range(1, grid.depth)]


def gather_x(grid, blocks):
    joined = jnp.stack(blocks)
    return joined, grid.send(joined, step_x=1)


def gather_all(grid, block):
    lines = gather_z(grid, block)
    return lines, list(gather_x(grid, lines))


def by_seq(first_value, second_value):
    return jnp.where(lax.axis_index("seq") == 0, first_value, second_value)


def gather_by_seq(grid, block, *beside):
    lines = gather_z(grid, by_seq(block[:1], block[1:]))
    joined, *beside = together(jnp.stack(lines), *beside)
    across = grid.send(joined, step_x=1)
    return lines, [joined, across, swap_seq(joined), swap_seq(across)], beside


def halves_of(left, right):
    going = contract_rows(left[1], right)
    return contract_rows(left[0], right), going


def add_pieces(kept, came, count):
    rows = kept.shape[0] // count
    return [
        (
            kept[step * rows : (step + 1) * rows].astype(f32)
            + came[step * rows : (step + 1) * rows].astype(f32)
        ).astype(bf16)
        for step in range(count)
    ]


def swap_seq(value):
    return lax.ppermute(value, "seq", [(0, 1), (1, 0)])


def sum_z(grid, sums):
    total = sums[0].astype(f32)
    for step in range(1, grid.depth):
        total = total + grid.send(sums[step], step_z=step).astype(f32)
    return total.astype(bf16)


class ScatterX:
    def __init__(self, grid, left, right):
        self.grid = grid
        self.kept, self.going = halves_of(left, right)
        self.came = grid.send(self.going, step_x=1)

    def add(self):
        self.sums = add_pieces(self.kept, self.came, self.grid.depth)
        return self.sums

    def finish(self):
        return sum_seq(sum_z(self.grid, self.sums))


class ScatterY:
    def __init__(self, grid, left, right):
        self.grid = grid
        self.kept, self.going = halves_of(left, right)
        self.came = swap_seq(self.going)

    def cross(self):
        self.kept, self.going = add_pieces(self.kept, self.came, 2)
        self.came = self.grid.send(self.going, step_x=1)
        return [self.kept, self.going]

    def add(self):
        self.sums = add_pieces(self.kept, self.came, self.grid.depth)
        return self.sums

    def finish(self):
        total = sum_z(self.grid, self.sums)
        other = swap_seq(total)
        first = lax.axis_index("seq") == 0
        return jnp.concatenate(
            [jnp.where(first, total, other), jnp.where(first, other, total)], axis=0
        ).astype(f32)


def sum_seq(value):
    groups = lax.axis_size("seq")
    if groups == 2:
        return value.astype(f32) + lax.ppermute(value, "seq", [(0, 1), (1, 0)]).astype(f32)
    return lax.psum(value.astype(f32), "seq")


def swap_twin(grid, total):
    rows = total.shape[0] // 2
    other = grid.send(total[rows:].astype(bf16), step_twin=1).astype(f32)
    return grid.in_order(total[:rows], other)


def sum_all(vector):
    for axis in ("fsdp", "seq"):
        count = lax.axis_size(axis)
        step = 1
        while step < count:
            vector = vector + lax.ppermute(
                vector, axis, [(member, member ^ step) for member in range(count)]
            )
            step *= 2
    return vector


def body(
    tokens,
    lengths,
    cotangent,
    attn_gain,
    attn_shift,
    qkv_weight,
    query_bias,
    value_bias,
    out_weight,
    out_bias,
    mlp_gain,
    mlp_shift,
    up_weight,
    up_bias,
    down_weight,
    down_bias,
):
    groups = lax.axis_size("seq")
    images, local_len, width = tokens.shape
    shard_rows = qkv_weight.shape[0]
    hidden_half = up_weight.shape[1] // 2
    rows = images * local_len
    heads = width // HD
    own_width = width // 2
    grid = Grid(shard_rows)
    all_members = jnp.stack(grid.members())

    def by_kind(matrix):
        lead = matrix.shape[0]
        split = matrix.reshape(lead, -1, heads // 2, 2, HD)
        return [split[:, :, :, kind].reshape(lead, -1) for kind in range(2)]

    def vector_kind(vector):
        return grid.own_half([vector.reshape(-1, 2, HD)[:, kind].reshape(-1) for kind in range(2)])

    def two_halves(matrix):
        return [matrix[:, :hidden_half], matrix[:, hidden_half:]]

    def pair_up(halves):
        other = grid.send(grid.other_half(halves), step_twin=1)
        return jnp.stack([grid.own_half(halves), other])

    def both(value):
        flat = value.reshape(rows, width)
        return jnp.concatenate([flat, grid.send(flat, step_twin=1)], axis=0)

    qkv_block = pair_up(by_kind(qkv_weight))
    all_kinds = jnp.stack(grid.shards())
    order = order_matrix(grid.shards(), shard_rows)
    own_order = order_matrix(grid.members(), shard_rows)
    inputs = both(tokens).astype(f32)
    normal_one, scale_one = norm_parts(inputs)
    normed_one = (normal_one * attn_gain + attn_shift).astype(bf16)
    qkv_block, up_weight, down_turned = together(qkv_block, up_weight, down_weight.T)
    pair_block, query_block = qkv_block[:, :, own_width:], qkv_block[:, :, :own_width]
    up_block = jnp.stack(grid.in_order(*pair_up(two_halves(up_weight))))
    down_block = jnp.stack(grid.in_order(*pair_up(two_halves(down_turned))))
    sizes = jnp.concatenate([lengths, grid.send(lengths, step_twin=1)])
    if groups == 2:
        scatter_seq, seq_order = ScatterY, order_matrix(grid.shards_by_seq(), shard_rows)
        pair_lines, pair_pieces, (normed_one, up_block, down_block, sizes) = gather_by_seq(
            grid, pair_block, normed_one, up_block, down_block, sizes
        )
        pair_slots = jnp.stack(grid.shards_by_seq())
    else:
        scatter_seq, seq_order = ScatterX, order
        pair_lines, pair_pieces = gather_all(grid, pair_block)
        pair_slots = all_kinds
    pair_pieces[1], query_block, down_block = together(pair_pieces[1], query_block, down_block)
    query_lines, query_pieces = gather_all(grid, query_block)
    query_pieces[1], out_block, up_block = together(query_pieces[1], out_weight[None], up_block)
    out_lines, out_pieces = gather_all(grid, out_block)

    if groups == 2:
        kinds_by_seq = jnp.stack(grid.kinds_by_seq())
        own_down = lax.all_gather(
            by_seq(down_block[0], down_block[1])[None],
            "fsdp",
            axis_index_groups=grid.groups(),
        )
        own_down = [own_down, swap_seq(own_down)]
    else:
        own_down = grid.gather(down_block)
    own_up = grid.gather(up_block)

    back_low = both(cotangent)

    own_pair = place(pair_pieces, pair_slots).reshape(width, 2 * own_width)
    pair_bias = jnp.concatenate([jnp.zeros((own_width,), f32), vector_kind(value_bias)])
    pairs = (jnp.dot(normed_one, own_pair, preferred_element_type=f32) + pair_bias).astype(bf16)
    pairs, row_source, back_source = together(pairs, normed_one, back_low)
    own_query = place(query_pieces, all_kinds)
    own_query = own_query.reshape(width, own_width)
    queries = (
        jnp.dot(normed_one, own_query, preferred_element_type=f32) + vector_kind(query_bias)
    ).astype(bf16)

    one_rows = reorder(row_source, order)
    seq_rows = reorder(row_source, seq_order) if groups == 2 else one_rows
    kind_rows = []
    if groups == 2:
        kind_rows = reorder(back_source, order_matrix(grid.kinds_by_seq(), shard_rows))
    made = [[*one_rows, *seq_rows, *kind_rows]] + [[]] * (2 * images - 1)
    if groups == 2:
        made[images] = [own_down[0]]

    place_seq = lax.axis_index("seq") * local_len
    attended_parts, saved = [], []
    for image in range(2 * images):
        span = slice(image * local_len, (image + 1) * local_len)
        query, near = queries[span][None], pairs[span][None]
        key, value = near[:, :, :own_width], near[:, :, own_width:]
        if groups == 2:
            far = swap_seq(near)
            key_parts = (key, far[:, :, :own_width])
            value_parts = (value, far[:, :, own_width:])
            info = jnp.stack([sizes[image], place_seq, local_len - place_seq])
        else:
            key_parts = (lax.all_gather(key, "seq", axis=1, tiled=True),)
            value_parts = (lax.all_gather(value, "seq", axis=1, tiled=True),)
            info = jnp.stack([sizes[image], jnp.zeros_like(sizes[image])])
        attended_part, lse = attend(
            info, query, key_parts, value_parts, made[image]
        )
        attended_parts.append(attended_part[0])
        saved.append((info, query, key_parts, value_parts, lse))
    attended = jnp.concatenate(attended_parts, axis=0)

    own_out = place(out_pieces, all_members)
    own_out = own_out.reshape(own_width, width)
    partial = jnp.dot(attended, own_out, preferred_element_type=f32)
    resid = inputs + partial + grid.swap_rows(partial, rows) + out_bias
    normal_two, scale_two = norm_parts(resid)
    normed_two = (normal_two * mlp_gain + mlp_shift).astype(bf16)
    own_up_bias = grid.own_half([up_bias[:hidden_half], up_bias[hidden_half:]])
    hidden = jnp.dot(normed_two, own_up, preferred_element_type=f32) + own_up_bias
    active, slope = gelu_and_slope(hidden)
    active, slope = together(active.astype(bf16), slope.astype(bf16))
    if groups == 2:
        active, own_down[1] = together(active, own_down[1])
    if groups == 2:
        down_kept, down_going = halves_of(kind_rows, active)
        down_came = swap_seq(down_going)
        own_down = place(own_down, kinds_by_seq, [down_kept, down_going])
        own_down = own_down.reshape(width, hidden_half)
    else:
        grad_down = grid.scatter(contract_rows(back_low, active))

    d_active = jnp.dot(back_low, own_down, preferred_element_type=f32)
    d_hidden = (d_active * slope).astype(bf16)
    grad_up = contract_rows(normed_two, d_hidden)
    d_hidden, grad_up = lax.optimization_barrier((d_hidden, grad_up))
    grad_up = grid.scatter(grad_up)
    partial = lax.dot_general(
        d_hidden, own_up, (((1,), (1,)), ((), ())), preferred_element_type=f32
    )
    d_two = partial + grid.swap_rows(partial, rows)
    d_resid = back_low.astype(f32) + norm_back(d_two, normal_two, scale_two, mlp_gain)
    out_low = d_resid.astype(bf16)
    grad_out = ScatterX(grid, reorder(attended, own_order), out_low)
    d_attended = lax.dot_general(
        out_low, own_out, (((1,), (1,)), ((), ())), preferred_element_type=f32
    ).astype(bf16)

    d_query, d_key, d_value = [], [], []
    for image in range(2 * images):
        span = slice(image * local_len, (image + 1) * local_len)
        info, query, key_parts, value_parts, lse = saved[image]
        if image == 0:
            on_their_way = [grad_out.kept, grad_out.going]
        elif image == images and groups == 2:
            on_their_way = add_pieces(down_kept, down_came, 1)
            down_total = on_their_way[0]
        else:
            on_their_way = []
        d_query_part, key_grads, value_grads = attend_back(
            info,
            query,
            d_attended[span][None],
            lse,
            key_parts,
            value_parts,
            on_their_way,
        )
        d_query.append(d_query_part[0])
        if groups == 2:
            near = jnp.concatenate([key_grads[1], value_grads[1]], axis=2)
            d_query[-1], near = together(d_query[-1], near)
            far = swap_seq(near)
            if image == 2 * images - 1:
                last_far = far
            d_key.append((key_grads[0], far[:, :, :own_width]))
            d_value.append((value_grads[0], far[:, :, own_width:]))
        else:
            for into, member in ((d_key, key_grads[0]), (d_value, value_grads[0])):
                into.append(
                    (
                        lax.psum_scatter(
                            member.astype(f32), "seq", scatter_dimension=1, tiled=True
                        ),
                    )
                )
    d_query = jnp.concatenate(d_query, axis=0)
    grad_query = ScatterX(grid, one_rows, d_query)
    late_active, grad_query.kept, grad_query.going = together(
        active, grad_query.kept, grad_query.going
    )
    partial = lax.dot_general(
        late_active, own_down, (((1,), (1,)), ((), ())), preferred_element_type=f32
    )
    came = grid.send(partial[rows:].astype(bf16), step_twin=1).astype(f32)
    outputs = (resid[:rows] + partial[:rows] + came + down_bias).astype(bf16)
    grad_query.add()
    if groups == 2:
        last_far, *grad_query.sums = together(last_far, *grad_query.sums)
        d_key[-1] = (d_key[-1][0], last_far[:, :, :own_width])
        d_value[-1] = (d_value[-1][0], last_far[:, :, own_width:])

    d_key, d_value = (
        jnp.concatenate(
            [sum(part.astype(f32) for part in parts)[0].astype(bf16) for parts in member], axis=0
        )
        for member in (d_key, d_value)
    )
    grad_key = scatter_seq(grid, seq_rows, d_key)
    grad_value = ScatterX(grid, one_rows, d_value)
    d_query, d_key, d_value, grad_key.kept, grad_key.going, grad_value.kept, grad_value.going = (
        together(
            d_query,
            d_key,
            d_value,
            grad_key.kept,
            grad_key.going,
            grad_value.kept,
            grad_value.going,
        )
    )
    partial = sum(
        lax.dot_general(member, weight, (((1,), (1,)), ((), ())), preferred_element_type=f32)
        for member, weight in (
            (d_query, own_query),
            (d_key, own_pair[:, :own_width]),
            (d_value, own_pair[:, own_width:]),
        )
    )
    d_one = partial[:rows] + grid.send(partial[rows:].astype(bf16), step_twin=1).astype(f32)
    d_one, grad_value.came, grad_up = together(d_one, grad_value.came, grad_up)
    grad_value.add()
    if groups == 2:
        grad_key.cross()
    (grad_out.came, grad_out.kept, *grad_value.sums) = together(
        grad_out.came, grad_out.kept, *grad_value.sums
    )
    grad_out.add()
    grad_tokens = d_resid[:rows] + norm_back(d_one, normal_one[:rows], scale_one[:rows], attn_gain)
    grad_key.add()
    grad_out = grad_out.finish()
    grad_up = sum_seq(grad_up)
    if groups == 2:
        grad_down = lax.psum_scatter(
            down_total,
            "fsdp",
            scatter_dimension=0,
            axis_index_groups=grid.groups(),
            tiled=True,
        )
        grad_down, *grad_key.sums = together(grad_down, *grad_key.sums)
        other = swap_seq(grad_down)
        grad_down = by_seq(
            jnp.concatenate([grad_down, other]), jnp.concatenate([other, grad_down])
        ).astype(f32)
    else:
        grad_down = sum_seq(grad_down)
    grad_qkv = jnp.concatenate(
        [grad_query.finish(), grad_key.finish(), grad_value.finish()], axis=1
    )

    grad_up, grad_down = (
        jnp.concatenate(grid.swap_mine(total[:shard_rows], total[shard_rows:]), axis=1)
        for total in (grad_up, grad_down)
    )
    grad_down = grad_down.T
    grad_qkv = jnp.stack(
        [member.reshape(shard_rows, 3, heads // 2, HD) for member in swap_twin(grid, grad_qkv)],
        axis=3,
    ).reshape(shard_rows, 3 * width)

    def at_kind(vector, shape, axis):
        vector = vector.reshape(shape)
        nothing = jnp.zeros_like(vector)
        return jnp.stack(grid.in_order(vector, nothing), axis=axis).reshape(-1)

    vectors = sum_all(
        jnp.concatenate(
            [
                column_sum(d_one * normal_one[:rows]),
                column_sum(d_one),
                at_kind(column_sum(d_query), (heads // 2, HD), 1),
                at_kind(column_sum(d_value), (heads // 2, HD), 1),
                column_sum(out_low[:rows]),
                column_sum(d_two[:rows] * normal_two[:rows]),
                column_sum(d_two[:rows]),
                column_sum(back_low[:rows]),
                at_kind(column_sum(d_hidden), (-1,), 0),
            ]
        )
    )
    (
        grad_attn_gain,
        grad_attn_shift,
        grad_query_bias,
        grad_value_bias,
        grad_out_bias,
        grad_mlp_gain,
        grad_mlp_shift,
        grad_down_bias,
    ) = (vectors[step * width : (step + 1) * width] for step in range(8))
    grad_up_bias = vectors[8 * width :]
    shape = (images, local_len, width)
    return (
        outputs.reshape(shape),
        grad_tokens.reshape(shape),
        grad_attn_gain,
        grad_attn_shift,
        grad_qkv,
        grad_query_bias,
        grad_value_bias,
        grad_out,
        grad_out_bias,
        grad_mlp_gain,
        grad_mlp_shift,
        grad_up,
        grad_up_bias,
        grad_down,
        grad_down_bias,
    )


def solution(mesh):
    return jax.shard_map(
        body,
        mesh=mesh,
        in_specs=(
            P("fsdp", "seq", None),
            P("fsdp"),
            P("fsdp", "seq", None),
            P(),
            P(),
            P("fsdp", None),
            P(),
            P(),
            P("fsdp", None),
            P(),
            P(),
            P(),
            P("fsdp", None),
            P(),
            P(None, "fsdp"),
            P(),
        ),
        out_specs=(
            P("fsdp", "seq", None),
            P("fsdp", "seq", None),
            P(),
            P(),
            P("fsdp", None),
            P(),
            P(),
            P("fsdp", None),
            P(),
            P(),
            P(),
            P("fsdp", None),
            P(),
            P(None, "fsdp"),
            P(),
        ),
        check_vma=False,
    )
```

```python
import functools

import jax
import jax.numpy as jnp
from jax import lax
from jax.experimental import pallas as pl
from jax.experimental.pallas import tpu as pltpu
from jax.sharding import PartitionSpec as P

HD = 72
WIDE = 128
SCALE = HD ** (-0.5)
masked_score = -1e30
epsilon = 1e-06
f32, bf16 = jnp.float32, jnp.bfloat16


def spread_heads(source, target, heads):
    for head in range(heads):
        target[head, :, :HD] = source[0, :, head * HD : (head + 1) * HD]


def turn_heads(source, target, heads):
    for head in range(heads):
        target[head] = jnp.transpose(source[head])


def join_heads(source, heads):
    return jnp.concatenate([source[head, :, :HD] for head in range(heads)], axis=1)


def nt(left, right):
    return lax.dot_general(left, right, (((1,), (1,)), ((), ())), preferred_element_type=f32)


def nn(left, right):
    return jnp.dot(left, right, preferred_element_type=f32)


def attend_kernel(parts, heads, block, earlier, info, *refs):
    q_in = refs[0]
    k_in = refs[1 : 1 + parts]
    v_in = refs[1 + parts : 1 + 2 * parts]
    refs = refs[1 + 2 * parts + earlier :]
    out, lse = refs[:2]
    scratch = refs[2:]
    q_s, o_s = scratch[:2]
    k_s = scratch[2 : 2 + parts]
    vt_s = scratch[2 + parts : 2 + 2 * parts]
    head = pl.program_id(0)
    rows = q_s.shape[1]

    @pl.when(head == 0)
    def _():
        q_s[...] = jnp.zeros_like(q_s)
        spread_heads(q_in, q_s, heads)
        for part in range(parts):
            k_s[part][...] = jnp.zeros_like(k_s[part])
            spread_heads(v_in[part], k_s[part], heads)
            turn_heads(k_s[part], vt_s[part], heads)
            spread_heads(k_in[part], k_s[part], heads)

    masks = []
    for part in range(parts):
        length = k_s[part].shape[1]
        masks.append(
            info[1 + part] + lax.broadcasted_iota(jnp.int32, (length, 1), 0) < info[0]
        )
    for start in range(0, rows, block):
        q_rows = q_s[head, start : start + block]
        scores = [
            jnp.where(masks[part], nt(k_s[part][head], q_rows), masked_score)
            for part in range(parts)
        ]
        peak = functools.reduce(
            jnp.maximum, [jnp.max(member, axis=0, keepdims=True) for member in scores]
        )
        total = 0.0
        result = 0.0
        for part in range(parts):
            grown = jnp.exp((scores[part] - peak) * SCALE)
            total = total + jnp.sum(grown, axis=0, keepdims=True)
            result = result + nn(vt_s[part][head], grown.astype(bf16))
        result = result / total
        o_s[head, start : start + block] = jnp.transpose(result).astype(bf16)
        lse[0, :, start : start + block] = peak * SCALE + jnp.log(total)

    @pl.when(head == heads - 1)
    def _():
        out[0] = join_heads(o_s, heads)


def attend_back_kernel(parts, heads, block, earlier, info, *refs):
    q_in, d_in, lse = refs[:3]
    k_in = refs[3 : 3 + parts]
    v_in = refs[3 + parts : 3 + 2 * parts]
    refs = refs[3 + 2 * parts + earlier :]
    dq_out = refs[0]
    dk_out = refs[1 : 1 + parts]
    dv_out = refs[1 + parts : 1 + 2 * parts]
    refs = refs[1 + 2 * parts :]
    q_s, d_s, dq_s = refs[:3]
    refs = refs[3:]
    k_s, v_s, kt_s, dk_s, dv_s = (refs[i * parts : (i + 1) * parts] for i in range(5))
    head = pl.program_id(0)
    rows = q_s.shape[1]

    @pl.when(head == 0)
    def _():
        q_s[...] = jnp.zeros_like(q_s)
        d_s[...] = jnp.zeros_like(d_s)
        spread_heads(q_in, q_s, heads)
        spread_heads(d_in, d_s, heads)
        for part in range(parts):
            k_s[part][...] = jnp.zeros_like(k_s[part])
            v_s[part][...] = jnp.zeros_like(v_s[part])
            spread_heads(k_in[part], k_s[part], heads)
            spread_heads(v_in[part], v_s[part], heads)
            turn_heads(k_s[part], kt_s[part], heads)

    masks = []
    for part in range(parts):
        length = k_s[part].shape[1]
        masks.append(
            info[1 + part] + lax.broadcasted_iota(jnp.int32, (length, 1), 0) < info[0]
        )
    d_key = [0.0] * parts
    d_value = [0.0] * parts
    for start in range(0, rows, block):
        q_rows = q_s[head, start : start + block]
        d_rows = d_s[head, start : start + block]
        level = lse[0, :, start : start + block]
        probs = []
        d_probs = []
        row_dot = 0.0
        for part in range(parts):
            scores = jnp.where(masks[part], nt(k_s[part][head], q_rows) * SCALE, masked_score)
            probs.append(jnp.exp(scores - level))
            d_probs.append(nt(v_s[part][head], d_rows))
            row_dot = row_dot + jnp.sum(probs[part] * d_probs[part], axis=0, keepdims=True)
        d_query = 0.0
        for part in range(parts):
            d_scores = (probs[part] * (d_probs[part] - row_dot)).astype(bf16)
            d_value[part] = d_value[part] + nn(probs[part].astype(bf16), d_rows)
            d_key[part] = d_key[part] + nn(d_scores, q_rows)
            d_query = d_query + nn(kt_s[part][head], d_scores)
        dq_s[head, start : start + block] = jnp.transpose(d_query * SCALE).astype(bf16)
    for part in range(parts):
        dk_s[part][head] = (d_key[part] * SCALE).astype(bf16)
        dv_s[part][head] = d_value[part].astype(bf16)

    @pl.when(head == heads - 1)
    def _():
        dq_out[0] = join_heads(dq_s, heads)
        for part in range(parts):
            dk_out[part][0] = join_heads(dk_s[part], heads)
            dv_out[part][0] = join_heads(dv_s[part], heads)


def whole(shape):
    return pl.BlockSpec(shape, lambda head: (0,) * len(shape))


def anywhere(arrays):
    return [pl.BlockSpec(memory_space=pl.ANY)] * len(arrays)


def attend(info, query, keys, values, earlier=(), block=512):
    _, rows, width = query.shape
    heads = width // HD
    parts = len(keys)
    lengths = [member.shape[1] for member in keys]
    total = sum(lengths)
    return pl.pallas_call(
        functools.partial(attend_kernel, parts, heads, min(block, rows), len(earlier)),
        grid=(heads,),
        in_specs=[pl.BlockSpec(memory_space=pltpu.SMEM), whole(query.shape)]
        + [whole(member.shape) for member in (*keys, *values)]
        + anywhere(earlier),
        out_specs=[whole(query.shape), pl.BlockSpec((1, 1, rows), lambda head: (head, 0, 0))],
        out_shape=[
            jax.ShapeDtypeStruct(query.shape, bf16),
            jax.ShapeDtypeStruct((heads, 1, rows), f32),
        ],
        scratch_shapes=[pltpu.VMEM((heads, rows, WIDE), bf16)] * 2
        + [pltpu.VMEM((heads, length, WIDE), bf16) for length in lengths]
        + [pltpu.VMEM((heads, WIDE, length), bf16) for length in lengths],
        compiler_params=pltpu.CompilerParams(vmem_limit_bytes=48 * 1024 * 1024),
        cost_estimate=pl.CostEstimate(
            flops=4 * heads * rows * total * 256,
            bytes_accessed=4 * (rows + total) * width,
            transcendentals=heads * rows * total,
        ),
    )(info, query, *keys, *values, *earlier)


def attend_back(info, query, d_out, lse, keys, values, earlier=(), block=256):
    _, rows, width = query.shape
    heads = width // HD
    parts = len(keys)
    lengths = [member.shape[1] for member in keys]
    total = sum(lengths)
    results = pl.pallas_call(
        functools.partial(attend_back_kernel, parts, heads, min(block, rows), len(earlier)),
        grid=(heads,),
        in_specs=[
            pl.BlockSpec(memory_space=pltpu.SMEM),
            whole(query.shape),
            whole(query.shape),
            pl.BlockSpec((1, 1, rows), lambda head: (head, 0, 0)),
        ]
        + [whole(member.shape) for member in (*keys, *values)]
        + anywhere(earlier),
        out_specs=[whole(member.shape) for member in (query, *keys, *values)],
        out_shape=[
            jax.ShapeDtypeStruct(member.shape, bf16) for member in (query, *keys, *values)
        ],
        scratch_shapes=[pltpu.VMEM((heads, rows, WIDE), bf16)] * 3
        + [pltpu.VMEM((heads, length, WIDE), bf16) for length in lengths] * 2
        + [pltpu.VMEM((heads, WIDE, length), bf16) for length in lengths]
        + [pltpu.VMEM((heads, length, WIDE), bf16) for length in lengths] * 2,
        compiler_params=pltpu.CompilerParams(vmem_limit_bytes=56 * 1024 * 1024),
        cost_estimate=pl.CostEstimate(
            flops=10 * heads * rows * total * 256,
            bytes_accessed=8 * (rows + total) * width,
            transcendentals=heads * rows * total,
        ),
    )(info, query, d_out, lse, *keys, *values, *earlier)
    return results[0], results[1 : 1 + parts], results[1 + parts :]


def contract_kernel(left, right, out, turned):
    @pl.when(pl.program_id(0) == 0)
    def _():
        turned[...] = jnp.transpose(left[...])

    out[...] = nn(turned[...], right[...]).astype(bf16)


def contract_rows(left, right, block=512):
    rows, width = left.shape
    columns = right.shape[1]
    block = min(block, columns)
    return pl.pallas_call(
        contract_kernel,
        grid=(pl.cdiv(columns, block),),
        in_specs=[
            pl.BlockSpec((rows, width), lambda step: (0, 0)),
            pl.BlockSpec((rows, block), lambda step: (0, step)),
        ],
        out_specs=pl.BlockSpec((width, block), lambda step: (0, step)),
        out_shape=jax.ShapeDtypeStruct((width, columns), bf16),
        scratch_shapes=[pltpu.VMEM((width, rows), bf16)],
        compiler_params=pltpu.CompilerParams(vmem_limit_bytes=40 * 1024 * 1024),
        cost_estimate=pl.CostEstimate(
            flops=2 * rows * width * columns,
            bytes_accessed=2 * (rows * width + (rows + width) * columns),
            transcendentals=0,
        ),
    )(left, right)


def column_sum(tensor):
    return jnp.sum(tensor.astype(f32), axis=0)


def after(value, *earlier):
    return lax.optimization_barrier((value, *earlier))[0]


def together(*values):
    return lax.optimization_barrier(values)


def norm_parts(tensor):
    centered = tensor - jnp.mean(tensor, axis=-1, keepdims=True)
    scale = lax.rsqrt(jnp.mean(centered * centered, axis=-1, keepdims=True) + epsilon)
    return centered * scale, scale


def norm_back(upstream, normal, scale, gain):
    weighted = upstream * gain
    mean_one = jnp.mean(weighted, axis=-1, keepdims=True)
    mean_two = jnp.mean(weighted * normal, axis=-1, keepdims=True)
    return scale * (weighted - mean_one - normal * mean_two)


def gelu_and_slope(tensor):
    square = tensor * tensor
    bent = jnp.tanh(0.7978845608028654 * tensor * (1.0 + 0.044715 * square))
    half = 0.5 * (1.0 + bent)
    slope = half + 0.5 * tensor * (1.0 - bent * bent) * 0.7978845608028654 * (
        1.0 + 0.134145 * square
    )
    return tensor * half, slope


def place_kernel(count, slots, *refs):
    pieces, (out, sems) = refs[:count], refs[-2:]
    copies = []
    for piece in pieces:
        for line in range(piece.shape[0]):
            for part in range(piece.shape[1]):
                index = len(copies)
                copies.append(
                    pltpu.make_async_copy(
                        piece.at[line, part], out.at[slots[index]], sems.at[index]
                    )
                )
    for copy in copies:
        copy.start()
    for copy in copies:
        copy.wait()


def place(pieces, slots, earlier=()):
    rows, columns = pieces[0].shape[2:]
    total = sum(piece.shape[0] * piece.shape[1] for piece in pieces)
    return pl.pallas_call(
        functools.partial(place_kernel, len(pieces)),
        in_specs=[pl.BlockSpec(memory_space=pltpu.SMEM)]
        + anywhere(pieces)
        + anywhere(earlier),
        out_specs=pl.BlockSpec(memory_space=pltpu.VMEM),
        out_shape=jax.ShapeDtypeStruct((total, rows, columns), pieces[0].dtype),
        scratch_shapes=[pltpu.SemaphoreType.DMA((total,))],
        compiler_params=pltpu.CompilerParams(vmem_limit_bytes=32 * 1024 * 1024),
        cost_estimate=pl.CostEstimate(
            flops=0, bytes_accessed=4 * total * rows * columns, transcendentals=0
        ),
    )(slots, *pieces, *earlier)


class Grid:
    def __init__(self, shard_rows):
        self.size = lax.axis_size("fsdp")
        self.apart = HD // shard_rows
        self.depth = self.size // 4
        me = lax.axis_index("fsdp")
        self.twin = (me // self.apart) % 2
        member = (me // (2 * self.apart)) * self.apart + me % self.apart
        self.z, self.x = member // 2, member % 2

    def index(self, z, x, twin):
        member = z * 2 + x
        return (
            (member // self.apart) * 2 * self.apart + twin * self.apart + member % self.apart
        )

    def pairs(self, step_z=0, step_x=0, step_twin=0):
        return [
            (
                self.index(z, x, twin),
                self.index((z + step_z) % self.depth, x ^ step_x, twin ^ step_twin),
            )
            for z in range(self.depth)
            for x in range(2)
            for twin in range(2)
        ]

    def send(self, value, **steps):
        return lax.ppermute(value, "fsdp", self.pairs(**steps))

    def members(self):
        return [
            ((self.z + step_z) % self.depth) * 2 + (self.x ^ step_x)
            for step_x in range(2)
            for step_z in range(self.depth)
        ]

    def shards(self):
        return [
            (member // self.apart) * 2 * self.apart
            + (self.twin ^ step) * self.apart
            + member % self.apart
            for member in self.members()
            for step in range(2)
        ]

    def kinds_by_seq(self):
        kinds = [
            [self.index(member // 2, member % 2, twin) for member in range(2 * self.depth)]
            for twin in range(2)
        ]
        first = lax.axis_index("seq") == 0
        return [jnp.where(first, one, two) for one, two in zip(*kinds)] + [
            jnp.where(first, two, one) for one, two in zip(*kinds)
        ]

    def shards_by_seq(self):
        mine = self.shards()
        first = lax.axis_index("seq") == 0
        kinds = [mine[0::2], mine[1::2]]
        return [jnp.where(first, one, two) for one, two in zip(*kinds)] + [
            jnp.where(first, two, one) for one, two in zip(*kinds)
        ]

    def groups(self):
        return [
            [self.index(member // 2, member % 2, twin) for member in range(2 * self.depth)]
            for twin in range(2)
        ]

    def gather(self, block):
        whole = lax.all_gather(block, "fsdp", axis_index_groups=self.groups())
        _, _, rows, columns = whole.shape
        whole = whole.reshape(-1, self.apart, 2, rows, columns).transpose(0, 2, 1, 3, 4)
        return whole.reshape(-1, columns)

    def scatter(self, matrix):
        columns = matrix.shape[1]
        matrix = matrix.reshape(2 * self.depth // self.apart, 2, self.apart, -1, columns)
        matrix = matrix.transpose(0, 2, 1, 3, 4).reshape(-1, columns)
        return lax.psum_scatter(
            matrix, "fsdp", scatter_dimension=0, axis_index_groups=self.groups(), tiled=True
        )

    def own_half(self, halves):
        return jnp.where(self.twin == 0, halves[0], halves[1])

    def other_half(self, halves):
        return jnp.where(self.twin == 0, halves[1], halves[0])

    def swap_rows(self, partial, rows):
        sent = jnp.concatenate([partial[rows:], partial[:rows]], axis=0).astype(bf16)
        return self.send(sent, step_twin=1).astype(f32)

    def swap_mine(self, first, second):
        mine, sent = self.in_order(first, second)
        return self.in_order(mine, self.send(sent.astype(bf16), step_twin=1).astype(f32))

    def in_order(self, mine, other):
        first = self.twin == 0
        return jnp.where(first, mine, other), jnp.where(first, other, mine)


def order_matrix(places, rows):
    count = len(places) * rows
    source = (jnp.stack(places) * rows)[:, None] + jnp.arange(rows, dtype=jnp.int32)[None, :]
    return (jnp.arange(count, dtype=jnp.int32)[:, None] == source.reshape(1, count)).astype(bf16)


def reorder(rows, matrix):
    half = matrix.shape[1] // 2
    return [
        jnp.dot(rows, part, preferred_element_type=f32).astype(bf16)
        for part in (matrix[:, :half], matrix[:, half:])
    ]


def gather_z(grid, block):
    sent = {step: grid.send(block, step_z=step) for step in range(1, grid.depth)}
    return [block] + [sent[grid.depth - step] for step in range(1, grid.depth)]


def gather_x(grid, blocks):
    joined = jnp.stack(blocks)
    return joined, grid.send(joined, step_x=1)


def gather_all(grid, block):
    lines = gather_z(grid, block)
    return lines, list(gather_x(grid, lines))


def by_seq(first_value, second_value):
    return jnp.where(lax.axis_index("seq") == 0, first_value, second_value)


def gather_by_seq(grid, block, *beside):
    lines = gather_z(grid, by_seq(block[:1], block[1:]))
    joined, *beside = together(jnp.stack(lines), *beside)
    across = grid.send(joined, step_x=1)
    return lines, [joined, across, swap_seq(joined), swap_seq(across)], beside


def halves_of(left, right):
    going = contract_rows(left[1], right)
    return contract_rows(left[0], right), going


def add_pieces(kept, came, count):
    rows = kept.shape[0] // count
    return [
        (
            kept[step * rows : (step + 1) * rows].astype(f32)
            + came[step * rows : (step + 1) * rows].astype(f32)
        ).astype(bf16)
        for step in range(count)
    ]


def swap_seq(value):
    return lax.ppermute(value, "seq", [(0, 1), (1, 0)])


def sum_z(grid, sums):
    total = sums[0].astype(f32)
    for step in range(1, grid.depth):
        total = total + grid.send(sums[step], step_z=step).astype(f32)
    return total.astype(bf16)


class ScatterX:
    def __init__(self, grid, left, right):
        self.grid = grid
        self.kept, self.going = halves_of(left, right)
        self.came = grid.send(self.going, step_x=1)

    def add(self):
        self.sums = add_pieces(self.kept, self.came, self.grid.depth)
        return self.sums

    def finish(self):
        return sum_seq(sum_z(self.grid, self.sums))


class ScatterY:
    def __init__(self, grid, left, right):
        self.grid = grid
        self.kept, self.going = halves_of(left, right)
        self.came = swap_seq(self.going)

    def cross(self):
        self.kept, self.going = add_pieces(self.kept, self.came, 2)
        self.came = self.grid.send(self.going, step_x=1)
        return [self.kept, self.going]

    def add(self):
        self.sums = add_pieces(self.kept, self.came, self.grid.depth)
        return self.sums

    def finish(self):
        total = sum_z(self.grid, self.sums)
        other = swap_seq(total)
        first = lax.axis_index("seq") == 0
        return jnp.concatenate(
            [jnp.where(first, total, other), jnp.where(first, other, total)], axis=0
        ).astype(f32)


def sum_seq(value):
    groups = lax.axis_size("seq")
    if groups == 2:
        return value.astype(f32) + lax.ppermute(value, "seq", [(0, 1), (1, 0)]).astype(f32)
    return lax.psum(value.astype(f32), "seq")


def swap_twin(grid, total):
    rows = total.shape[0] // 2
    other = grid.send(total[rows:].astype(bf16), step_twin=1).astype(f32)
    return grid.in_order(total[:rows], other)


def sum_all(vector):
    for axis in ("fsdp", "seq"):
        count = lax.axis_size(axis)
        step = 1
        while step < count:
            vector = vector + lax.ppermute(
                vector, axis, [(member, member ^ step) for member in range(count)]
            )
            step *= 2
    return vector


def body(
    tokens,
    lengths,
    cotangent,
    attn_gain,
    attn_shift,
    qkv_weight,
    query_bias,
    value_bias,
    out_weight,
    out_bias,
    mlp_gain,
    mlp_shift,
    up_weight,
    up_bias,
    down_weight,
    down_bias,
):
    groups = lax.axis_size("seq")
    images, local_len, width = tokens.shape
    shard_rows = qkv_weight.shape[0]
    hidden_half = up_weight.shape[1] // 2
    rows = images * local_len
    heads = width // HD
    own_width = width // 2
    grid = Grid(shard_rows)
    all_members = jnp.stack(grid.members())

    def by_kind(matrix):
        lead = matrix.shape[0]
        split = matrix.reshape(lead, -1, heads // 2, 2, HD)
        return [split[:, :, :, kind].reshape(lead, -1) for kind in range(2)]

    def vector_kind(vector):
        return grid.own_half([vector.reshape(-1, 2, HD)[:, kind].reshape(-1) for kind in range(2)])

    def two_halves(matrix):
        return [matrix[:, :hidden_half], matrix[:, hidden_half:]]

    def pair_up(halves):
        other = grid.send(grid.other_half(halves), step_twin=1)
        return jnp.stack([grid.own_half(halves), other])

    def both(value):
        flat = value.reshape(rows, width)
        return jnp.concatenate([flat, grid.send(flat, step_twin=1)], axis=0)

    qkv_block = pair_up(by_kind(qkv_weight))
    all_kinds = jnp.stack(grid.shards())
    order = order_matrix(grid.shards(), shard_rows)
    own_order = order_matrix(grid.members(), shard_rows)
    inputs = both(tokens).astype(f32)
    normal_one, scale_one = norm_parts(inputs)
    normed_one = (normal_one * attn_gain + attn_shift).astype(bf16)
    qkv_block, up_weight, down_turned = together(qkv_block, up_weight, down_weight.T)
    pair_block, query_block = qkv_block[:, :, own_width:], qkv_block[:, :, :own_width]
    up_block = jnp.stack(grid.in_order(*pair_up(two_halves(up_weight))))
    down_block = jnp.stack(grid.in_order(*pair_up(two_halves(down_turned))))
    sizes = jnp.concatenate([lengths, grid.send(lengths, step_twin=1)])
    if groups == 2:
        scatter_seq, seq_order = ScatterY, order_matrix(grid.shards_by_seq(), shard_rows)
        pair_lines, pair_pieces, (normed_one, up_block, down_block, sizes) = gather_by_seq(
            grid, pair_block, normed_one, up_block, down_block, sizes
        )
        pair_slots = jnp.stack(grid.shards_by_seq())
    else:
        scatter_seq, seq_order = ScatterX, order
        pair_lines, pair_pieces = gather_all(grid, pair_block)
        pair_slots = all_kinds
    pair_pieces[1], query_block, up_block = together(pair_pieces[1], query_block, up_block)
    query_lines, query_pieces = gather_all(grid, query_block)
    query_pieces[1], out_block, down_block = together(
        query_pieces[1], out_weight[None], down_block
    )
    out_lines, out_pieces = gather_all(grid, out_block)

    own_up, own_down = grid.gather(up_block), grid.gather(down_block)

    back_low = both(cotangent)

    own_pair = place(pair_pieces, pair_slots).reshape(width, 2 * own_width)
    pair_bias = jnp.concatenate([jnp.zeros((own_width,), f32), vector_kind(value_bias)])
    pairs = (jnp.dot(normed_one, own_pair, preferred_element_type=f32) + pair_bias).astype(bf16)
    pairs, row_source = together(pairs, normed_one)
    own_query = place(query_pieces, all_kinds)
    own_query = own_query.reshape(width, own_width)
    queries = (
        jnp.dot(normed_one, own_query, preferred_element_type=f32) + vector_kind(query_bias)
    ).astype(bf16)

    one_rows = reorder(row_source, order)
    seq_rows = reorder(row_source, seq_order) if groups == 2 else one_rows
    made = [[*one_rows, *seq_rows]] + [[]] * (2 * images - 1)

    place_seq = lax.axis_index("seq") * local_len
    attended_parts, saved = [], []
    for image in range(2 * images):
        span = slice(image * local_len, (image + 1) * local_len)
        query, near = queries[span][None], pairs[span][None]
        key, value = near[:, :, :own_width], near[:, :, own_width:]
        if groups == 2:
            far = swap_seq(near)
            key_parts = (key, far[:, :, :own_width])
            value_parts = (value, far[:, :, own_width:])
            info = jnp.stack([sizes[image], place_seq, local_len - place_seq])
        else:
            key_parts = (lax.all_gather(key, "seq", axis=1, tiled=True),)
            value_parts = (lax.all_gather(value, "seq", axis=1, tiled=True),)
            info = jnp.stack([sizes[image], jnp.zeros_like(sizes[image])])
        attended_part, lse = attend(
            info, query, key_parts, value_parts, made[image]
        )
        attended_parts.append(attended_part[0])
        saved.append((info, query, key_parts, value_parts, lse))
    attended = jnp.concatenate(attended_parts, axis=0)

    own_out = place(out_pieces, all_members, attended_parts[-1:])
    own_out = own_out.reshape(own_width, width)
    partial = jnp.dot(attended, own_out, preferred_element_type=f32)
    resid = inputs + partial + grid.swap_rows(partial, rows) + out_bias
    normal_two, scale_two = norm_parts(resid)
    normed_two = (normal_two * mlp_gain + mlp_shift).astype(bf16)
    own_up_bias = grid.own_half([up_bias[:hidden_half], up_bias[hidden_half:]])
    hidden = jnp.dot(normed_two, own_up, preferred_element_type=f32) + own_up_bias
    active, slope = gelu_and_slope(hidden)
    active, slope = together(active.astype(bf16), slope.astype(bf16))
    grad_down = contract_rows(back_low, active)
    back_low, grad_down = together(back_low, grad_down)
    grad_down = grid.scatter(grad_down)

    d_active = jnp.dot(back_low, own_down, preferred_element_type=f32)
    d_hidden = (d_active * slope).astype(bf16)
    grad_up = contract_rows(normed_two, d_hidden)
    d_hidden, grad_up = lax.optimization_barrier((d_hidden, grad_up))
    grad_up = grid.scatter(grad_up)
    partial = lax.dot_general(
        d_hidden, own_up, (((1,), (1,)), ((), ())), preferred_element_type=f32
    )
    d_two = partial + grid.swap_rows(partial, rows)
    d_resid = back_low.astype(f32) + norm_back(d_two, normal_two, scale_two, mlp_gain)
    out_low = d_resid.astype(bf16)
    grad_out = ScatterX(grid, reorder(attended, own_order), out_low)
    d_attended = lax.dot_general(
        out_low, own_out, (((1,), (1,)), ((), ())), preferred_element_type=f32
    ).astype(bf16)

    d_query, d_key, d_value = [], [], []
    for image in range(2 * images):
        span = slice(image * local_len, (image + 1) * local_len)
        info, query, key_parts, value_parts, lse = saved[image]
        if image == 0:
            on_their_way = [grad_out.kept, grad_out.going]
        else:
            on_their_way = []
        d_query_part, key_grads, value_grads = attend_back(
            info,
            query,
            d_attended[span][None],
            lse,
            key_parts,
            value_parts,
            on_their_way,
        )
        d_query.append(d_query_part[0])
        if groups == 2:
            near = jnp.concatenate([key_grads[1], value_grads[1]], axis=2)
            d_query[-1], near = together(d_query[-1], near)
            far = swap_seq(near)
            if image == 0:
                first_far = far
            if image == 2 * images - 1:
                last_far = far
            d_key.append((key_grads[0], far[:, :, :own_width]))
            d_value.append((value_grads[0], far[:, :, own_width:]))
        else:
            for into, member in ((d_key, key_grads[0]), (d_value, value_grads[0])):
                into.append(
                    (
                        lax.psum_scatter(
                            member.astype(f32), "seq", scatter_dimension=1, tiled=True
                        ),
                    )
                )
    d_query = jnp.concatenate(d_query, axis=0)
    if groups == 2:
        d_query, first_far = together(d_query, first_far)
        d_key[0] = (d_key[0][0], first_far[:, :, :own_width])
        d_value[0] = (d_value[0][0], first_far[:, :, own_width:])
    grad_query = ScatterX(grid, one_rows, d_query)
    late_active, grad_query.kept, grad_query.going = together(
        active, grad_query.kept, grad_query.going
    )
    partial = lax.dot_general(
        late_active, own_down, (((1,), (1,)), ((), ())), preferred_element_type=f32
    )
    came = grid.send(partial[rows:].astype(bf16), step_twin=1).astype(f32)
    outputs = (resid[:rows] + partial[:rows] + came + down_bias).astype(bf16)
    if groups == 2:
        last_far, grad_down = together(last_far, grad_down)
        d_key[-1] = (d_key[-1][0], last_far[:, :, :own_width])
        d_value[-1] = (d_value[-1][0], last_far[:, :, own_width:])

    d_key, d_value = (
        jnp.concatenate(
            [sum(part.astype(f32) for part in parts)[0].astype(bf16) for parts in member], axis=0
        )
        for member in (d_key, d_value)
    )
    grad_key = scatter_seq(grid, seq_rows, d_key)
    grad_value = ScatterX(grid, one_rows, d_value)
    d_query, d_key, d_value, grad_key.kept, grad_key.going, grad_value.kept, grad_value.going = (
        together(
            d_query,
            d_key,
            d_value,
            grad_key.kept,
            grad_key.going,
            grad_value.kept,
            grad_value.going,
        )
    )
    partial = sum(
        lax.dot_general(member, weight, (((1,), (1,)), ((), ())), preferred_element_type=f32)
        for member, weight in (
            (d_query, own_query),
            (d_key, own_pair[:, :own_width]),
            (d_value, own_pair[:, own_width:]),
        )
    )
    d_one = partial[:rows] + grid.send(partial[rows:].astype(bf16), step_twin=1).astype(f32)
    grad_down = sum_seq(grad_down)
    grad_out.came, grad_query.came, grad_key.came, grad_value.came, grad_down = together(
        grad_out.came, grad_query.came, grad_key.came, grad_value.came, grad_down
    )
    grad_out.add()
    grad_query.add()
    grad_value.add()
    if groups == 2:
        grad_key.cross()
    grad_tokens = d_resid[:rows] + norm_back(d_one, normal_one[:rows], scale_one[:rows], attn_gain)
    grad_key.add()
    grad_out = grad_out.finish()
    grad_up = sum_seq(grad_up)
    grad_qkv = jnp.concatenate(
        [grad_query.finish(), grad_key.finish(), grad_value.finish()], axis=1
    )

    grad_qkv = jnp.stack(
        [member.reshape(shard_rows, 3, heads // 2, HD) for member in swap_twin(grid, grad_qkv)],
        axis=3,
    ).reshape(shard_rows, 3 * width)

    def at_kind(vector, shape, axis):
        vector = vector.reshape(shape)
        nothing = jnp.zeros_like(vector)
        return jnp.stack(grid.in_order(vector, nothing), axis=axis).reshape(-1)

    vectors = jnp.concatenate(
            [
                column_sum(d_one * normal_one[:rows]),
                column_sum(d_one),
                at_kind(column_sum(d_query), (heads // 2, HD), 1),
                at_kind(column_sum(d_value), (heads // 2, HD), 1),
                column_sum(out_low[:rows]),
                column_sum(d_two[:rows] * normal_two[:rows]),
                column_sum(d_two[:rows]),
                column_sum(back_low[:rows]),
                at_kind(column_sum(d_hidden), (-1,), 0),
            ]
        )
    vectors, grad_up = together(vectors, grad_up)
    vectors = sum_all(vectors)
    grad_up, grad_down = (
        jnp.concatenate(grid.swap_mine(total[:shard_rows], total[shard_rows:]), axis=1)
        for total in (grad_up, grad_down)
    )
    grad_down = grad_down.T
    (
        grad_attn_gain,
        grad_attn_shift,
        grad_query_bias,
        grad_value_bias,
        grad_out_bias,
        grad_mlp_gain,
        grad_mlp_shift,
        grad_down_bias,
    ) = (vectors[step * width : (step + 1) * width] for step in range(8))
    grad_up_bias = vectors[8 * width :]
    shape = (images, local_len, width)
    return (
        outputs.reshape(shape),
        grad_tokens.reshape(shape),
        grad_attn_gain,
        grad_attn_shift,
        grad_qkv,
        grad_query_bias,
        grad_value_bias,
        grad_out,
        grad_out_bias,
        grad_mlp_gain,
        grad_mlp_shift,
        grad_up,
        grad_up_bias,
        grad_down,
        grad_down_bias,
    )


def solution(mesh):
    return jax.shard_map(
        body,
        mesh=mesh,
        in_specs=(
            P("fsdp", "seq", None),
            P("fsdp"),
            P("fsdp", "seq", None),
            P(),
            P(),
            P("fsdp", None),
            P(),
            P(),
            P("fsdp", None),
            P(),
            P(),
            P(),
            P("fsdp", None),
            P(),
            P(None, "fsdp"),
            P(),
        ),
        out_specs=(
            P("fsdp", "seq", None),
            P("fsdp", "seq", None),
            P(),
            P(),
            P("fsdp", None),
            P(),
            P(),
            P("fsdp", None),
            P(),
            P(),
            P(),
            P("fsdp", None),
            P(),
            P(None, "fsdp"),
            P(),
        ),
        check_vma=False,
    )
```
